32 devices in a mesh: dom: 8 (over z, core), grp: 4 (over y, x).
Axes of the slice: x: 2, y: 2, z: 4, core: 2. Of those that a mesh axis runs over, the one named last changes fastest.
Arguments:
- node_latent: bfloat16 [32768, 128], P(('dom', 'grp')), may hold values from -6 to 6
- node_tangent: bfloat16 [32768, 128], P(('dom', 'grp')), may hold values from -6 to 6
- edge_latent: bfloat16 [131072, 128], P(('dom', 'grp')), may hold values from -6 to 6
- node_counts: int32 [32], P(('dom', 'grp')), may hold values from 512 to 1024, as said below
- edge_counts: int32 [32], P(('dom', 'grp')), may hold values from 2048 to 4096, as said below
- send_lists: int32 [32, 4, 128], P(('dom', 'grp')), may hold values from 0 to 1023, as said below
- edge_source: int32 [32, 4096], P(('dom', 'grp')), may hold values from 0 to 1535, as said below
- edge_target: int32 [32, 4096], P(('dom', 'grp')), may hold values from 0 to 1023, as said below
- coarse_owner: int32 [32, 1024], P(('dom', 'grp')), may hold values from 0 to 127
- coarse_source: int32 [1024, 8], P(('dom', 'grp')), may hold values from 0 to 383, as said below
- edge_first: bfloat16 [384, 128], replicated, may hold values from -0.3125 to 0.3125
- edge_second: bfloat16 [128, 128], replicated, may hold values from -0.5 to 0.5
- node_first: bfloat16 [256, 128], replicated, may hold values from -0.375 to 0.375
- node_second: bfloat16 [128, 128], replicated, may hold values from -0.5 to 0.5
- message_first: bfloat16 [256, 128], replicated, may hold values from -0.375 to 0.375
- message_second: bfloat16 [128, 128], replicated, may hold values from -0.5 to 0.5
- coarse_first: bfloat16 [256, 128], replicated, may hold values from -0.375 to 0.375
- coarse_second: bfloat16 [128, 128], replicated, may hold values from -0.5 to 0.5
- prolong_first: bfloat16 [256, 128], replicated, may hold values from -0.375 to 0.375
- prolong_second: bfloat16 [128, 128], replicated, may hold values from -0.5 to 0.5
Outputs:
- node_output: bfloat16 [32768, 128], P(('dom', 'grp'))
- tangent_output: bfloat16 [32768, 128], P(('dom', 'grp'))
The draws below stay inside these ranges and needn't reach their ends.
Inputs may be any that keep to these rules, and one draw needn't show every extreme that they name: node_counts[p] is at least half of 1024; some partition has all 1024 slots valid. edge_counts[p] is at least half of 4096; some partition has all 4096 slots valid. `send_lists`: every entry is a valid node row of its own partition (below node_counts[p]). `edge_source`: every entry is either a valid node row of the partition (below node_counts[p]) or a halo row 1024 + r with r < 512. `edge_target`: every entry is a valid node row of the partition. `coarse_source`: entries below 32 * 4 name nodes of row d-1, entries from 2 * 32 * 4 on name nodes of row d+1, the others nodes of row d itself.
All inputs are finite; a program needn't handle non-finite values.
Results may differ from the reference program's by a relative error of at most 0.012.
Values may be sent and summed in bfloat16 or wider, within the bound.
No kernel may reach another device: no remote copies, remote signals or barrier semaphores. Data moves between devices by JAX's collectives and lax.ppermute only.
A program may use at most 64 MiB of HBM per device.

```python
import jax
import jax.numpy as jnp
from jax import lax

L = 128
NF_DEV = 1024
E_DEV = 4096
HALO = 128
NC_DEV = 32
KC = 8
PARTS_SIZE = 32
NF = 32768
E = 131072
NC = 1024
N_DOM = 8
N_GRP = 4


def count_table(key, salt, most):
    drawn = jax.random.randint(jax.random.fold_in(key, salt), (PARTS_SIZE,), most // 2, most + 1)
    chosen = jax.random.randint(jax.random.fold_in(key, salt + 1), (), 0, PARTS_SIZE)
    return jnp.where(jnp.arange(PARTS_SIZE) == chosen, most, drawn).astype(jnp.int32)


def draw_node_counts(key, part):
    return count_table(key, 11, NF_DEV)


def draw_edge_counts(key, part):
    return count_table(key, 31, E_DEV)


def draw_send_lists(key, part):
    nodes = count_table(key, 11, NF_DEV)
    return jax.random.randint(jax.random.fold_in(key, 51), (PARTS_SIZE, 4, HALO), 0, nodes[:, None, None]).astype(jnp.int32)


def draw_edge_source(key, part):
    nodes = count_table(key, 11, NF_DEV)[:, None]
    picked = jax.random.randint(jax.random.fold_in(key, 61), (PARTS_SIZE, E_DEV), 0, nodes + 4 * HALO)
    return jnp.where(picked < nodes, picked, picked - nodes + NF_DEV).astype(jnp.int32)


def draw_edge_target(key, part):
    nodes = count_table(key, 11, NF_DEV)[:, None]
    return jax.random.randint(jax.random.fold_in(key, 71), (PARTS_SIZE, E_DEV), 0, nodes).astype(jnp.int32)


def draw_coarse_source(key, part):
    row_nodes = NC_DEV * N_GRP
    within = jax.random.randint(jax.random.fold_in(key, 81), (NC, KC), 0, row_nodes)
    outside = jax.random.randint(jax.random.fold_in(key, 82), (NC, KC), 0, 4) == 0
    upper = jax.random.randint(jax.random.fold_in(key, 83), (NC, KC), 0, 2)
    return jnp.where(outside, within + 2 * row_nodes * upper, within + row_nodes).astype(jnp.int32)


def place_ends(result, rng, smallest, largest):
    shape = result.shape
    index_at = [jax.random.randint(jax.random.fold_in(rng, axis), (), 0, shape[axis]) for axis in range(len(shape))]
    result = result.at[tuple(index_at)].set(smallest)
    longest = shape.index(max(shape))
    index_at[longest] = (index_at[longest] + 1) % shape[longest]
    return result.at[tuple(index_at)].set(largest)


def block_levels(key, dims, split, low, largest):
    level, own = 1.0, jax.random.fold_in(key, 6)
    for axis_at, shards_of in split:
        steps = jnp.exp(jax.random.uniform(jax.random.fold_in(own, axis_at), (shards_of,), jnp.float32, low / len(split), largest / len(split)))
        level = level * jnp.repeat(steps, dims[axis_at] // shards_of).reshape([-1 if axis == axis_at else 1 for axis in range(len(dims))])
    return level


def scatter_about(stream_key, dims, width, limit, shards=(), kind=jnp.bfloat16):
    values = width * jax.random.normal(stream_key, dims, jnp.float32)
    if shards:
        values = values * block_levels(stream_key, dims, shards, -0.22, 0.18)
    return jnp.clip(values, -limit, limit).astype(kind)


def setup_inputs(seed: int = 0) -> dict:
    seeds = jax.random.split(jax.random.key(seed), 21)
    node_latent = scatter_about(seeds[0], (NF, L), 1.0, 6.0, ((0, 32),))
    node_tangent = scatter_about(seeds[1], (NF, L), 1.0, 6.0, ((0, 32),))
    edge_latent = scatter_about(seeds[2], (E, L), 1.0, 6.0, ((0, 32),))
    node_counts = draw_node_counts(jax.random.fold_in(seeds[20], 71), 0)
    edge_counts = draw_edge_counts(jax.random.fold_in(seeds[20], 71), 0)
    send_lists = draw_send_lists(jax.random.fold_in(seeds[20], 71), 0)
    edge_source = draw_edge_source(jax.random.fold_in(seeds[20], 71), 0)
    edge_target = draw_edge_target(jax.random.fold_in(seeds[20], 71), 0)
    coarse_owner = place_ends(jax.random.randint(seeds[8], (PARTS_SIZE, NF_DEV), 0, NC_DEV * N_GRP), jax.random.fold_in(seeds[8], 1), 0, (NC_DEV * N_GRP) - 1).astype(jnp.int32)
    coarse_source = draw_coarse_source(jax.random.fold_in(seeds[20], 71), 0)
    edge_first = scatter_about(seeds[10], (3 * L, L), (3 * L) ** -0.5, 0.3125)
    edge_second = scatter_about(seeds[11], (L, L), L ** -0.5, 0.5)
    node_first = scatter_about(seeds[12], (2 * L, L), (2 * L) ** -0.5, 0.375)
    node_second = scatter_about(seeds[13], (L, L), L ** -0.5, 0.5)
    message_first = scatter_about(seeds[14], (2 * L, L), (2 * L) ** -0.5, 0.375)
    message_second = scatter_about(seeds[15], (L, L), L ** -0.5, 0.5)
    coarse_first = scatter_about(seeds[16], (2 * L, L), (2 * L) ** -0.5, 0.375)
    coarse_second = scatter_about(seeds[17], (L, L), L ** -0.5, 0.5)
    prolong_first = scatter_about(seeds[18], (2 * L, L), (2 * L) ** -0.5, 0.375)
    prolong_second = scatter_about(seeds[19], (L, L), L ** -0.5, 0.5)
    return {"node_latent": node_latent, "node_tangent": node_tangent, "edge_latent": edge_latent, "node_counts": node_counts, "edge_counts": edge_counts, "send_lists": send_lists, "edge_source": edge_source, "edge_target": edge_target, "coarse_owner": coarse_owner, "coarse_source": coarse_source, "edge_first": edge_first, "edge_second": edge_second, "node_first": node_first, "node_second": node_second, "message_first": message_first, "message_second": message_second, "coarse_first": coarse_first, "coarse_second": coarse_second, "prolong_first": prolong_first, "prolong_second": prolong_second}


def layer_norm(value):
    centred = value - lax.optimization_barrier(jnp.mean(value, axis=-1, keepdims=True))
    spread = lax.optimization_barrier(jnp.mean(centred * centred, axis=-1, keepdims=True))
    return centred * lax.rsqrt(spread + 1e-05)

def perceptron(inputs, first, second):
    hidden = jax.nn.silu(jnp.dot(inputs, first, preferred_element_type=jnp.float32)).astype(jnp.bfloat16)
    return jnp.dot(hidden, second, preferred_element_type=jnp.float32)

def edge_update(edges, source, target, first, second):
    joined = jnp.concatenate([edges, source, target], axis=-1)
    return (edges.astype(jnp.float32) + layer_norm(perceptron(joined, first, second))).astype(jnp.bfloat16)

def node_update(nodes, other, first, second):
    joined = jnp.concatenate([nodes, other], axis=-1)
    return (nodes.astype(jnp.float32) + layer_norm(perceptron(joined, first, second))).astype(jnp.bfloat16)

def coarse_update(table, sources, mine, weights):
    message_first, message_second, coarse_first, coarse_second = weights
    senders = table[sources]
    receivers = jnp.broadcast_to(mine[:, None, :], senders.shape)
    joined = jnp.concatenate([senders, receivers], axis=-1).reshape(-1, 2 * senders.shape[-1])
    terms = perceptron(joined, message_first, message_second).reshape(senders.shape)
    message = lax.optimization_barrier(jnp.sum(terms, axis=1)).astype(jnp.bfloat16)
    joined = jnp.concatenate([mine, message], axis=-1)
    return layer_norm(perceptron(joined, coarse_first, coarse_second)).astype(jnp.bfloat16)

def from_lower(block, axis):
    empty = jnp.zeros_like(lax.slice_in_dim(block, 0, 1, axis=axis))
    return jnp.concatenate([empty, lax.slice_in_dim(block, 0, block.shape[axis] - 1, axis=axis)], axis=axis)

def from_upper(block, axis):
    empty = jnp.zeros_like(lax.slice_in_dim(block, 0, 1, axis=axis))
    return jnp.concatenate([lax.slice_in_dim(block, 1, block.shape[axis], axis=axis), empty], axis=axis)

def reference(node_latent, node_tangent, edge_latent, node_counts, edge_counts, send_lists, edge_source, edge_target, coarse_owner, coarse_source, edge_first, edge_second, node_first, node_second, message_first, message_second, coarse_first, coarse_second, prolong_first, prolong_second):
    paired = jnp.concatenate([node_latent, node_tangent], axis=1).reshape(N_DOM, N_GRP, NF_DEV, 2 * L)
    lists = send_lists.reshape(N_DOM, N_GRP, 4 * HALO)
    sent = jax.vmap(jax.vmap(lambda rows, picks: rows[picks]))(paired, lists).reshape(N_DOM, N_GRP, 4, HALO, 2 * L)
    halo = jnp.stack([from_lower(sent[:, :, 0], 0), from_upper(sent[:, :, 1], 0), from_lower(sent[:, :, 2], 1), from_upper(sent[:, :, 3], 1)], axis=2)
    halo = halo.reshape(N_DOM * N_GRP, 4 * HALO, 2 * L)
    local = paired.reshape(N_DOM * N_GRP, NF_DEV, 2 * L)
    tables = jnp.concatenate([local, halo], axis=1)

    def fine_part(items):
        table, edges, source, target, edge_total = items
        sender = table[source]
        receiver = table[target]
        edge_new, edge_tan = jax.jvp(lambda a, b, c: edge_update(a, b, c, edge_first, edge_second), (edges, sender[:, :L], receiver[:, :L]), (jnp.zeros_like(edges), sender[:, L:], receiver[:, L:]))
        live = (jnp.arange(E_DEV) < edge_total)[:, None]
        agg = jax.ops.segment_sum(jnp.where(live, edge_new.astype(jnp.float32), 0.0), target, num_segments=NF_DEV).astype(jnp.bfloat16)
        agg_tan = jax.ops.segment_sum(jnp.where(live, edge_tan.astype(jnp.float32), 0.0), target, num_segments=NF_DEV).astype(jnp.bfloat16)
        nodes = table[:NF_DEV]
        first, first_tan = jax.jvp(lambda a, b: node_update(a, b, node_first, node_second), (nodes[:, :L], agg), (nodes[:, L:], agg_tan))
        return jnp.concatenate([first, first_tan], axis=1)
    firsts = lax.map(fine_part, (tables, edge_latent.reshape(N_DOM * N_GRP, E_DEV, L), edge_source, edge_target, edge_counts))
    valid = (jnp.arange(NF_DEV)[None, :] < node_counts[:, None])[:, :, None]
    masked = jnp.where(valid, firsts.astype(jnp.float32), 0.0).reshape(N_DOM, N_GRP * NF_DEV, 2 * L)
    owners = coarse_owner.reshape(N_DOM, N_GRP * NF_DEV)
    sums = jax.vmap(lambda values, keys: jax.ops.segment_sum(values, keys, num_segments=NC_DEV * N_GRP))(masked, owners)
    coarse = sums.astype(jnp.bfloat16)
    rows3 = jnp.concatenate([from_lower(coarse, 0), coarse, from_upper(coarse, 0)], axis=1)
    sources = coarse_source.reshape(N_DOM, NC_DEV * N_GRP, KC)
    weights = (message_first, message_second, coarse_first, coarse_second)

    def coarse_row(table, mine, row_sources):
        updated, updated_tan = jax.jvp(lambda a, b: coarse_update(a, row_sources, b, weights), (table[:, :L], mine[:, :L]), (table[:, L:], mine[:, L:]))
        return jnp.concatenate([updated, updated_tan], axis=1)
    updated = jax.vmap(coarse_row)(rows3, coarse, sources)
    pulled = jax.vmap(lambda rows, keys: rows[keys])(updated, owners).reshape(N_DOM * N_GRP, NF_DEV, 2 * L)

    def final_part(items):
        first, brought = items
        final, final_tan = jax.jvp(lambda a, b: node_update(a, b, prolong_first, prolong_second), (first[:, :L], brought[:, :L]), (first[:, L:], brought[:, L:]))
        return jnp.concatenate([final, final_tan], axis=1)
    finals = lax.map(final_part, (firsts, pulled))
    finals = jnp.where(valid, finals, jnp.zeros_like(finals)).reshape(N_DOM * N_GRP * NF_DEV, 2 * L)
    return (finals[:, :L], finals[:, L:])
```

```python
import functools

import jax
import jax.numpy as jnp
from jax import lax
from jax.experimental import pallas as pl
from jax.experimental.pallas import tpu as pltpu
from jax.sharding import PartitionSpec as P

BF = jnp.bfloat16
F32 = jnp.float32
I16 = jnp.int16
I32 = jnp.int32
ANY = pl.BlockSpec(memory_space=pl.ANY)
SMEM = pl.BlockSpec(memory_space=pltpu.SMEM)
VMEM = pl.BlockSpec(memory_space=pltpu.VMEM)
LANES = 128


def mm(a, b):
    return jnp.dot(a, b, preferred_element_type=F32)


def twice(weight):
    zero = jnp.zeros_like(weight)
    return jnp.concatenate(
        [jnp.concatenate([weight, zero], 1), jnp.concatenate([zero, weight], 1)], 0
    )


def centred(weight):
    weight = weight.astype(F32)
    return (weight - jnp.mean(weight, axis=1, keepdims=True)).astype(BF)


def averaging(width):
    return twice(jnp.full((width, width), 1.0 / width, BF))


def column(row):
    count = row.shape[1]
    parts = [
        jnp.broadcast_to(row[:, k : k + LANES], (LANES, LANES)).T for k in range(0, count, LANES)
    ]
    return jnp.concatenate(parts, 0).astype(I16)


def picks(col, count):
    lane = lax.broadcasted_iota(I32, (1, LANES), 1).astype(I16)
    one, zero = jnp.ones((), BF), jnp.zeros((), BF)
    return [
        jnp.where(col == jnp.broadcast_to(lane + jnp.asarray(k, I16), col.shape), one, zero)
        for k in range(0, count, LANES)
    ]


def row_picks(row, count):
    shape = (count, row.shape[1])
    return jnp.where(
        jnp.broadcast_to(row, shape).astype(I16) == lax.broadcasted_iota(I32, shape, 0).astype(I16),
        jnp.ones((), BF),
        jnp.zeros((), BF),
    )


def activated(pre):
    width = pre.shape[1] // 2
    value, tangent = pre[:, :width], pre[:, width:]
    gate = 1.0 / (1.0 + jnp.exp(-value))
    hidden = value * gate
    slope = gate + hidden * (1.0 - gate)
    return jnp.concatenate([hidden, tangent * slope], 1)


def normed(pre, second, ones):
    width = pre.shape[1] // 2
    both = mm(activated(pre).astype(BF), second)
    value, tangent = both[:, :width], both[:, width:]
    stats = mm(jnp.concatenate([value * value, value * tangent], 1).astype(BF), ones)
    scale = lax.rsqrt(stats[:, :width] + 1e-05)
    return value * scale, scale * (tangent - value * (scale * scale * stats[:, width:]))


def fetch(pairs, sems):
    copies = [pltpu.make_async_copy(src, dst, sems.at[k]) for k, (src, dst) in enumerate(pairs)]
    for copy in copies:
        copy.start()
    return copies


def halo_kernel(nl, nt, lists, o0, o1, o2, o3, nl_v, nt_v, lists_v, sems):
    for copy in fetch([(nl, nl_v), (nt, nt_v), (lists, lists_v)], sems):
        copy.wait()
    slots = nl.shape[0]
    paired = jnp.concatenate([nl_v[...], nt_v[...]], 1)
    even = (lax.rem(lax.axis_index("dom"), 2) == 0, lax.rem(lax.axis_index("grp"), 2) == 0)
    for k, out in enumerate((o0, o1, o2, o3)):
        base = k // 2 * 2
        up = even[k // 2] if k % 2 == 0 else jnp.logical_not(even[k // 2])
        row = jnp.where(up, lists_v[0, base : base + 1, :], lists_v[0, base + 1 : base + 2, :])
        selector = jnp.concatenate(picks(column(row), slots), 1)
        out[...] = mm(selector, paired).astype(BF)


def edge_kernel(nl, nt, ed, src, tgt, own, cs, nc, ec, h0, h1, h2, h3, ef, es, nf, ns,
                first_o, part_o,
                nl_v, nt_v, ed_v, src_v, tgt_v, own_v, cs_v, h0_v, h1_v, h2_v, h3_v, ef_v, es_v, nf_v, ns_v,
                table, total, second, ones, sems, *, block):
    copies = fetch(
        list(zip(
            (nl, nt, ef, h0, h1, h2, h3, src, tgt, es, ed, nf, ns, own, cs),
            (nl_v, nt_v, ef_v, h0_v, h1_v, h2_v, h3_v, src_v, tgt_v, es_v, ed_v, nf_v, ns_v, own_v, cs_v),
        )),
        sems,
    )
    for copy in copies:
        copy.wait()
    slots, width = nl.shape
    edges = ed.shape[0]
    rim = h0.shape[0]
    reach = slots + 4 * rim
    paired = jnp.concatenate([nl_v[...], nt_v[...]], 1)
    weight = twice(ef_v[width : 2 * width, :])
    table[0:slots, :] = mm(paired, weight).astype(BF)
    odd = (lax.rem(lax.axis_index("dom"), 2), lax.rem(lax.axis_index("grp"), 2))
    for k, got in enumerate((h0_v, h1_v, h2_v, h3_v)):
        place = k // 2 * 2 + (odd[k // 2] if k % 2 else 1 - odd[k // 2])
        at = pl.ds(pl.multiple_of(slots + place * rim, rim), rim)
        table[at, :] = mm(got[...], weight).astype(BF)
    table[reach:, :] = mm(paired, twice(ef_v[2 * width :, :])).astype(BF)
    second[...] = twice(centred(es_v[...]))
    ones[...] = averaging(width)
    total[...] = jnp.zeros_like(total)
    own_weight = ef_v[0:width, :]
    live = ec[0]

    def step(number, carry):
        at = pl.ds(pl.multiple_of(number * block, block), block)
        target = tgt_v[0:1, at]
        selector = jnp.concatenate(
            picks(column(src_v[0:1, at]), reach) + picks(column(target), slots), 1
        )
        pre = mm(selector, table[...])
        mine = ed_v[at, :]
        pre = jnp.concatenate([pre[:, :width] + mm(mine, own_weight), pre[:, width:]], 1)
        value, tangent = normed(pre, second[...], ones[...])
        pair = jnp.concatenate([mine.astype(F32) + value, tangent], 1).astype(BF)
        slot = lax.broadcasted_iota(I32, (1, block), 1) + number * block
        total[...] += mm(row_picks(jnp.where(slot < live, target, -1), slots), pair)
        return carry

    lax.fori_loop(0, edges // block, step, 0)
    pre = mm(paired, twice(nf_v[0:width, :])) + mm(total[...].astype(BF), twice(nf_v[width:, :]))
    value, tangent = normed(pre, twice(centred(ns_v[...])), ones[...])
    first = (paired.astype(F32) + jnp.concatenate([value, tangent], 1)).astype(BF)
    first_o[...] = first
    owner = own_v[...]
    owner = jnp.where(lax.broadcasted_iota(I32, owner.shape, 1) < nc[0], owner, -1)
    owned, fan = cs.shape
    row_nodes = owned * lax.axis_size("grp")
    part_o[0:row_nodes, :] = mm(row_picks(owner, row_nodes), first).astype(BF)
    high = (cs_v[...] // 256).astype(BF)
    low = lax.rem(cs_v[...], 256).astype(BF)
    lane = lax.broadcasted_iota(I32, (owned, 2 * width), 1)
    spot = lax.broadcasted_iota(I32, (owned, 2 * width), 0) + lax.axis_index("grp") * owned
    for k in range((part_o.shape[0] - row_nodes) // (2 * fan)):
        place = jnp.where(lane + k * 2 * width == spot, jnp.ones((), F32), jnp.zeros((), F32)).astype(BF)
        rows = [
            lax.dot_general(part, place, (((0,), (0,)), ((), ())), preferred_element_type=F32)
            for part in (high, low)
        ]
        base = row_nodes + k * 2 * fan
        part_o[base : base + 2 * fan, :] = jnp.concatenate(rows, 0).astype(BF)


def coarse_kernel(summed, v0, v1, first, own, nc, mf, ms, cf, cs, pf, ps,
                  node_o, tangent_o,
                  summed_v, v0_v, v1_v, first_v, own_v, mf_v, ms_v, cf_v, cs_v, pf_v, ps_v,
                  table, sems, *, row_nodes, fan):
    copies = fetch(
        list(zip(
            (mf, summed, v0, v1, ms, cf, cs, pf, ps, own, first),
            (mf_v, summed_v, v0_v, v1_v, ms_v, cf_v, cs_v, pf_v, ps_v, own_v, first_v),
        )),
        sems,
    )
    for copy in copies:
        copy.wait()
    slots, width = node_o.shape
    ones = averaging(width)
    mine = summed_v[0:row_nodes, :]
    weight = twice(mf_v[0:width, :])
    table[row_nodes : 2 * row_nodes, :] = mm(mine, weight).astype(BF)
    odd = lax.rem(lax.axis_index("dom"), 2)
    for k, got in enumerate((v0_v, v1_v)):
        place = 2 * odd if k else 2 - 2 * odd
        at = pl.ds(pl.multiple_of(place * row_nodes, row_nodes), row_nodes)
        table[at, :] = mm(got[0:row_nodes, :], weight).astype(BF)
    received = mm(mine, twice(mf_v[width:, :]))
    sums = []
    for begin in range(0, row_nodes, LANES):
        chunk, lanes = divmod(begin, 2 * width)
        base = row_nodes + chunk * 2 * fan
        spots = summed_v[base : base + 2 * fan, lanes : lanes + LANES].astype(F32)
        spots = (spots[0:fan, :] * 256.0 + spots[fan:, :]).astype(I32)
        got = received[begin : begin + LANES, :]
        selector = jnp.concatenate([column(spots[j : j + 1, :]) for j in range(fan)], 0)
        pre = mm(jnp.concatenate(picks(selector, 3 * row_nodes), 1), table[...])
        hidden = activated(pre + jnp.concatenate([got] * fan, 0))
        sums.append(sum(hidden[j * LANES : (j + 1) * LANES, :] for j in range(fan)))
    hidden = jnp.concatenate(sums, 0)
    weight = twice(ms_v[...])
    large = hidden.astype(BF)
    message = (mm(large, weight) + mm((hidden - large.astype(F32)).astype(BF), weight)).astype(BF)
    pre = mm(mine, twice(cf_v[0:width, :])) + mm(message, twice(cf_v[width:, :]))
    value, tangent = normed(pre, twice(centred(cs_v[...])), ones)
    updated = jnp.concatenate([value, tangent], 1).astype(BF)
    brought = mm(updated, twice(pf_v[width:, :])).astype(BF)
    owner = jnp.concatenate(picks(column(own_v[...]), row_nodes), 1)
    first_all = first_v[...]
    pre = mm(first_all, twice(pf_v[0:width, :])) + mm(owner, brought)
    value, tangent = normed(pre, twice(centred(ps_v[...])), ones)
    valid = lax.broadcasted_iota(I32, (slots, 1), 0) < nc[0]
    node_o[...] = jnp.where(valid, first_all[:, :width].astype(F32) + value, 0.0).astype(BF)
    tangent_o[...] = jnp.where(valid, first_all[:, width:].astype(F32) + tangent, 0.0).astype(BF)


def like(*arrays):
    return [pltpu.VMEM(a.shape, a.dtype) for a in arrays]


def params():
    return pltpu.CompilerParams(vmem_limit_bytes=48 * 2**20)


def swap(x, axis, first):
    pairs = []
    for i in range(first, lax.axis_size(axis) - 1, 2):
        pairs += [(i, i + 1), (i + 1, i)]
    return lax.ppermute(x, axis, pairs)


def row_sum(x):
    size = lax.axis_size("grp")
    total = x.astype(F32)
    for by in range(1, size):
        if size & (size - 1) == 0:
            pairs = [(i, i ^ by) for i in range(size)]
        else:
            pairs = [(i, (i + by) % size) for i in range(size)]
        total = total + lax.ppermute(x, "grp", pairs).astype(F32)
    return total.astype(BF)


def per_device(nl, nt, ed, nc, ec, lists, src, tgt, own, sources, ef, es, nf, ns, mf, ms, cf, cs, pf, ps):
    slots, width = nl.shape
    edges = ed.shape[0]
    rim = lists.shape[2]
    owned, fan = sources.shape
    row_nodes = owned * lax.axis_size("grp")
    extra = 2 * fan * (-(-row_nodes // (2 * width)))
    shape = jax.ShapeDtypeStruct
    sent = pl.pallas_call(
        halo_kernel,
        out_shape=[shape((rim, 2 * width), BF)] * 4,
        in_specs=[ANY] * 3,
        out_specs=[VMEM] * 4,
        scratch_shapes=like(nl, nt, lists) + [pltpu.SemaphoreType.DMA((3,))],
        compiler_params=params(),
        name="halo_rows",
    )(nl, nt, lists)
    got = [swap(sent[k], ("dom", "grp")[k // 2], k % 2) for k in range(4)]
    first, part = pl.pallas_call(
        functools.partial(edge_kernel, block=min(edges, 1024)),
        out_shape=[shape((slots, 2 * width), BF), shape((row_nodes + extra, 2 * width), BF)],
        in_specs=[ANY] * 7 + [SMEM] * 2 + [ANY] * 8,
        out_specs=[VMEM] * 2,
        scratch_shapes=like(nl, nt, ed, src, tgt, own, sources, *got, ef, es, nf, ns)
        + [
            pltpu.VMEM((2 * slots + 4 * rim, 2 * width), BF),
            pltpu.VMEM((slots, 2 * width), F32),
            pltpu.VMEM((2 * width, 2 * width), BF),
            pltpu.VMEM((2 * width, 2 * width), BF),
            pltpu.SemaphoreType.DMA((15,)),
        ],
        compiler_params=params(),
        name="edges",
    )(nl, nt, ed, src, tgt, own, sources, nc, ec, *got, ef, es, nf, ns)
    summed = row_sum(part)
    v0, v1 = swap(summed, "dom", 0), swap(summed, "dom", 1)
    return pl.pallas_call(
        functools.partial(coarse_kernel, row_nodes=row_nodes, fan=fan),
        out_shape=[shape((slots, width), BF)] * 2,
        in_specs=[ANY] * 5 + [SMEM] + [ANY] * 6,
        out_specs=[VMEM] * 2,
        scratch_shapes=like(summed, v0, v1, first, own, mf, ms, cf, cs, pf, ps)
        + [pltpu.VMEM((3 * row_nodes, 2 * width), BF), pltpu.SemaphoreType.DMA((11,))],
        compiler_params=params(),
        name="coarse",
    )(summed, v0, v1, first, own, nc, mf, ms, cf, cs, pf, ps)


def solution(mesh):
    parts = ("dom", "grp")
    rows = P(parts, None)
    in_specs = (rows,) * 3 + (P(parts),) * 2 + (P(parts, None, None),) + (rows,) * 4 + (P(),) * 10
    return jax.shard_map(
        per_device, mesh=mesh, in_specs=in_specs, out_specs=(rows, rows), check_vma=False
    )
```

```python
import functools

import jax
import jax.numpy as jnp
from jax import lax
from jax.experimental import pallas as pl
from jax.experimental.pallas import tpu as pltpu
from jax.sharding import PartitionSpec as P

BF = jnp.bfloat16
F32 = jnp.float32
I16 = jnp.int16
I32 = jnp.int32
HBM = pl.BlockSpec(memory_space=pltpu.HBM)
SMEM = pl.BlockSpec(memory_space=pltpu.SMEM)
VMEM = pl.BlockSpec(memory_space=pltpu.VMEM)
LANES = 128


def mm(a, b):
    return jnp.dot(a, b, preferred_element_type=F32)


def twice(weight):
    zero = jnp.zeros_like(weight)
    return jnp.concatenate(
        [jnp.concatenate([weight, zero], 1), jnp.concatenate([zero, weight], 1)], 0
    )


def centred(weight):
    weight = weight.astype(F32)
    return (weight - jnp.mean(weight, axis=1, keepdims=True)).astype(BF)


def averaging(width):
    return twice(jnp.full((width, width), 1.0 / width, BF))


def column(row):
    count = row.shape[1]
    parts = [
        jnp.broadcast_to(row[:, k : k + LANES], (LANES, LANES)).T for k in range(0, count, LANES)
    ]
    return jnp.concatenate(parts, 0).astype(I16)


def picks(col, count):
    lane = lax.broadcasted_iota(I32, (1, LANES), 1).astype(I16)
    one, zero = jnp.ones((), BF), jnp.zeros((), BF)
    return [
        jnp.where(col == jnp.broadcast_to(lane + jnp.asarray(k, I16), col.shape), one, zero)
        for k in range(0, count, LANES)
    ]


def row_picks(row, count):
    shape = (count, row.shape[1])
    return jnp.where(
        jnp.broadcast_to(row, shape).astype(I16) == lax.broadcasted_iota(I32, shape, 0).astype(I16),
        jnp.ones((), BF),
        jnp.zeros((), BF),
    )


def activated(pre):
    width = pre.shape[1] // 2
    value, tangent = pre[:, :width], pre[:, width:]
    gate = 1.0 / (1.0 + jnp.exp(-value))
    hidden = value * gate
    slope = gate + hidden * (1.0 - gate)
    return jnp.concatenate([hidden, tangent * slope], 1)


def normed(pre, second, ones):
    width = pre.shape[1] // 2
    both = mm(activated(pre).astype(BF), second)
    value, tangent = both[:, :width], both[:, width:]
    stats = mm(jnp.concatenate([value * value, value * tangent], 1).astype(BF), ones)
    scale = lax.rsqrt(stats[:, :width] + 1e-05)
    return value * scale, scale * (tangent - value * (scale * scale * stats[:, width:]))


def fetch(pairs, sems):
    copies = [pltpu.make_async_copy(src, dst, sems.at[k]) for k, (src, dst) in enumerate(pairs)]
    for copy in copies:
        copy.start()
    return copies


def halo_kernel(nl, nt, lists, o0, o1, o2, o3, nl_v, nt_v, lists_v, sems):
    for copy in fetch([(nl, nl_v), (nt, nt_v), (lists, lists_v)], sems):
        copy.wait()
    slots = nl.shape[0]
    paired = jnp.concatenate([nl_v[...], nt_v[...]], 1)
    even = (lax.rem(lax.axis_index("dom"), 2) == 0, lax.rem(lax.axis_index("grp"), 2) == 0)
    for k, out in enumerate((o0, o1, o2, o3)):
        base = k // 2 * 2
        up = even[k // 2] if k % 2 == 0 else jnp.logical_not(even[k // 2])
        row = jnp.where(up, lists_v[0, base : base + 1, :], lists_v[0, base + 1 : base + 2, :])
        selector = jnp.concatenate(picks(column(row), slots), 1)
        out[...] = mm(selector, paired).astype(BF)


def local_kernel(nl, nt, src, tgt, ef, pre_o, nl_v, nt_v, src_v, tgt_v, ef_v, table, pre_v, sems, out_sems, *, block):
    copies = fetch([(nl, nl_v), (nt, nt_v), (ef, ef_v), (src, src_v), (tgt, tgt_v)], sems)
    for copy in copies:
        copy.wait()
    slots, width = nl.shape
    paired = jnp.concatenate([nl_v[...], nt_v[...]], 1)
    table[0:slots, :] = mm(paired, twice(ef_v[width : 2 * width, :])).astype(BF)
    table[slots:, :] = mm(paired, twice(ef_v[2 * width :, :])).astype(BF)
    stores = []
    for k, begin in enumerate(range(0, pre_o.shape[0], block)):
        at = slice(begin, begin + block)
        selector = jnp.concatenate(
            picks(column(src_v[0:1, at]), slots) + picks(column(tgt_v[0:1, at]), slots), 1
        )
        pre_v[at, :] = mm(selector, table[...])
        copy = pltpu.make_async_copy(pre_v.at[at], pre_o.at[at], out_sems.at[k])
        copy.start()
        stores.append(copy)
    for copy in stores:
        copy.wait()


def edge_kernel(nl, nt, ed, src, tgt, own, sources, ef, es, nf, ns, nc, ec, h0, h1, h2, h3, pre,
                first_o, part_o,
                nl_v, nt_v, ed_v, src_v, tgt_v, own_v, sources_v, ef_v, es_v, nf_v, ns_v,
                table, pairs, pre_v, sems, pre_sems, *, block, rows):
    copies = fetch(
        list(zip(
            (ef, src, es, ed, tgt, nl, nt, nf, ns, own, sources),
            (ef_v, src_v, es_v, ed_v, tgt_v, nl_v, nt_v, nf_v, ns_v, own_v, sources_v),
        )),
        sems,
    )
    slots, width = nl.shape
    edges = ed.shape[0]
    rim = h0.shape[0]
    cuts = [slice(begin, begin + block) for begin in range(0, edges, block)]
    given_copies = fetch([(pre.at[at], pre_v.at[at]) for at in cuts], pre_sems)
    for copy in copies[:3]:
        copy.wait()
    weight = twice(ef_v[width : 2 * width, :])
    odd = (lax.rem(lax.axis_index("dom"), 2), lax.rem(lax.axis_index("grp"), 2))
    for k, got in enumerate((h0, h1, h2, h3)):
        place = k // 2 * 2 + (odd[k // 2] if k % 2 else 1 - odd[k // 2])
        at = pl.ds(pl.multiple_of(place * rim, rim), rim)
        table[at, :] = mm(got[...], weight).astype(BF)
    second = twice(centred(es_v[...]))
    ones = averaging(width)
    own_weight = ef_v[0:width, :]
    for copy in copies[3:]:
        copy.wait()
    for at, copy in zip(cuts, given_copies):
        copy.wait()
        selector = jnp.concatenate(picks(column(src_v[0:1, at] - slots), 4 * rim), 1)
        mine = ed_v[at, :]
        given = pre_v[at, :] + mm(selector, table[...])
        given = jnp.concatenate([given[:, :width] + mm(mine, own_weight), given[:, width:]], 1)
        value, tangent = normed(given, second, ones)
        pairs[at, :] = jnp.concatenate([mine.astype(F32) + value, tangent], 1).astype(BF)
    target = jnp.where(lax.broadcasted_iota(I32, (1, edges), 1) < ec[0], tgt_v[...], -1)
    owner = jnp.where(lax.broadcasted_iota(I32, (1, slots), 1) < nc[0], own_v[...], -1)
    fixed = twice(nf_v[0:width, :])
    added = twice(nf_v[width:, :])
    second = twice(centred(ns_v[...]))
    fan, owned = sources.shape
    row_nodes = owned * lax.axis_size("grp")
    part = jnp.zeros((row_nodes, 2 * width), F32)
    for begin in range(0, slots, rows):
        at = slice(begin, begin + rows)
        agg = mm(row_picks(target - begin, rows), pairs[...]).astype(BF)
        paired = jnp.concatenate([nl_v[at, :], nt_v[at, :]], 1)
        value, tangent = normed(mm(paired, fixed) + mm(agg, added), second, ones)
        first = (paired.astype(F32) + jnp.concatenate([value, tangent], 1)).astype(BF)
        first_o[at, :] = first
        part = part + mm(row_picks(owner[:, at], row_nodes), first)
    part_o[0:row_nodes, :] = part.astype(BF)
    high = (sources_v[...] // 256).astype(F32).astype(BF)
    low = lax.rem(sources_v[...], 256).astype(F32).astype(BF)
    lane = lax.broadcasted_iota(I32, (owned, 2 * width), 1)
    spot = lax.broadcasted_iota(I32, (owned, 2 * width), 0) + lax.axis_index("grp") * owned
    for k in range((part_o.shape[0] - row_nodes) // (2 * fan)):
        place = jnp.where(lane + k * 2 * width == spot, jnp.ones((), F32), jnp.zeros((), F32)).astype(BF)
        base = row_nodes + k * 2 * fan
        part_o[base : base + 2 * fan, :] = jnp.concatenate([mm(high, place), mm(low, place)], 0).astype(BF)


def coarse_kernel(summed, v0, v1, first, nc, own, mf, ms, cf, cs, pf, ps,
                  node_o, tangent_o,
                  own_v, mf_v, ms_v, cf_v, cs_v, pf_v, ps_v,
                  table, node_v, tangent_v, sems, out_sems, *, row_nodes, fan, rows):
    copies = fetch(
        list(zip(
            (mf, ms, cf, cs, pf, ps, own),
            (mf_v, ms_v, cf_v, cs_v, pf_v, ps_v, own_v),
        )),
        sems,
    )
    for copy in copies:
        copy.wait()
    slots, width = node_o.shape
    ones = averaging(width)
    mine = summed[0:row_nodes, :]
    weight = twice(mf_v[0:width, :])
    table[row_nodes : 2 * row_nodes, :] = mm(mine, weight).astype(BF)
    odd = lax.rem(lax.axis_index("dom"), 2)
    for k, got in enumerate((v0, v1)):
        place = 2 * odd if k else 2 - 2 * odd
        at = pl.ds(pl.multiple_of(place * row_nodes, row_nodes), row_nodes)
        table[at, :] = mm(got[0:row_nodes, :], weight).astype(BF)
    received = mm(mine, twice(mf_v[width:, :]))
    sums = []
    for begin in range(0, row_nodes, LANES):
        chunk, lanes = divmod(begin, 2 * width)
        base = row_nodes + chunk * 2 * fan
        spots = summed[base : base + 2 * fan, lanes : lanes + LANES].astype(F32)
        spots = (spots[0:fan, :] * 256.0 + spots[fan:, :]).astype(I32)
        got = received[begin : begin + LANES, :]
        selector = jnp.concatenate([column(spots[j : j + 1, :]) for j in range(fan)], 0)
        pre = mm(jnp.concatenate(picks(selector, 3 * row_nodes), 1), table[...])
        hidden = activated(pre + jnp.concatenate([got] * fan, 0))
        sums.append(sum(hidden[j * LANES : (j + 1) * LANES, :] for j in range(fan)))
    hidden = jnp.concatenate(sums, 0)
    weight = twice(ms_v[...])
    large = hidden.astype(BF)
    message = (mm(large, weight) + mm((hidden - large.astype(F32)).astype(BF), weight)).astype(BF)
    pre = mm(mine, twice(cf_v[0:width, :])) + mm(message, twice(cf_v[width:, :]))
    value, tangent = normed(pre, twice(centred(cs_v[...])), ones)
    updated = jnp.concatenate([value, tangent], 1).astype(BF)
    brought = mm(updated, twice(pf_v[width:, :])).astype(BF)
    fixed = twice(pf_v[0:width, :])
    second = twice(centred(ps_v[...]))
    stores = []
    for k, begin in enumerate(range(0, slots, rows)):
        at = slice(begin, begin + rows)
        selector = jnp.concatenate(picks(column(own_v[:, at]), row_nodes), 1)
        block = first[at, :]
        value, tangent = normed(mm(block, fixed) + mm(selector, brought), second, ones)
        valid = lax.broadcasted_iota(I32, (rows, 1), 0) + begin < nc[0]
        node_v[at, :] = jnp.where(valid, block[:, :width].astype(F32) + value, 0.0).astype(BF)
        tangent_v[at, :] = jnp.where(valid, block[:, width:].astype(F32) + tangent, 0.0).astype(BF)
        for i, (held, out) in enumerate(((node_v, node_o), (tangent_v, tangent_o))):
            copy = pltpu.make_async_copy(held.at[at], out.at[at], out_sems.at[2 * k + i])
            copy.start()
            stores.append(copy)
    for copy in stores:
        copy.wait()


def like(*arrays):
    return [pltpu.VMEM(a.shape, a.dtype) for a in arrays]


def params(mib=40):
    return pltpu.CompilerParams(vmem_limit_bytes=int(mib * 2**20))


def swap(x, axis, first):
    pairs = []
    for i in range(first, lax.axis_size(axis) - 1, 2):
        pairs += [(i, i + 1), (i + 1, i)]
    return lax.ppermute(x, axis, pairs)


def row_sum(x):
    size = lax.axis_size("grp")
    total = x.astype(F32)
    for by in range(1, size):
        if size & (size - 1) == 0:
            pairs = [(i, i ^ by) for i in range(size)]
        else:
            pairs = [(i, (i + by) % size) for i in range(size)]
        total = total + lax.ppermute(x, "grp", pairs).astype(F32)
    return total.astype(BF)


def per_device(nl, nt, ed, nc, ec, lists, src, tgt, own, sources, ef, es, nf, ns, mf, ms, cf, cs, pf, ps):
    slots, width = nl.shape
    edges = ed.shape[0]
    rim = lists.shape[2]
    owned, fan = sources.shape
    sources = sources.T
    row_nodes = owned * lax.axis_size("grp")
    extra = 2 * fan * (-(-row_nodes // (2 * width)))
    rows, block = min(slots, 256), min(edges, 512)
    shape = jax.ShapeDtypeStruct
    dma = pltpu.SemaphoreType.DMA
    sent = pl.pallas_call(
        halo_kernel,
        out_shape=[shape((rim, 2 * width), BF)] * 4,
        in_specs=[HBM] * 3,
        out_specs=[VMEM] * 4,
        scratch_shapes=like(nl, nt, lists) + [dma((3,))],
        compiler_params=params(60),
        name="halo_rows",
    )(nl, nt, lists)
    got = [swap(sent[k], ("dom", "grp")[k // 2], k % 2) for k in range(4)]
    pre = pl.pallas_call(
        functools.partial(local_kernel, block=block),
        out_shape=shape((edges, 2 * width), F32),
        in_specs=[HBM] * 5,
        out_specs=HBM,
        scratch_shapes=like(nl, nt, src, tgt, ef)
        + [
            pltpu.VMEM((2 * slots, 2 * width), BF),
            pltpu.VMEM((edges, 2 * width), F32),
            dma((5,)),
            dma((edges // block,)),
        ],
        compiler_params=params(59),
        cost_estimate=pl.CostEstimate(
            flops=8 * edges * slots * width, bytes_accessed=8 * edges * width, transcendentals=0
        ),
        name="local",
    )(nl, nt, src, tgt, ef)
    first, part = pl.pallas_call(
        functools.partial(edge_kernel, block=block, rows=rows),
        out_shape=[shape((slots, 2 * width), BF), shape((row_nodes + extra, 2 * width), BF)],
        in_specs=[HBM] * 11 + [SMEM] * 2 + [VMEM] * 4 + [HBM],
        out_specs=[VMEM] * 2,
        scratch_shapes=like(nl, nt, ed, src, tgt, own, sources)
        + like(ef, es, nf, ns)
        + [pltpu.VMEM((4 * rim, 2 * width), BF), pltpu.VMEM((edges, 2 * width), BF), pltpu.VMEM((edges, 2 * width), F32)]
        + [dma((11,)), dma((edges // block,))],
        compiler_params=params(51),
        name="edges",
    )(nl, nt, ed, src, tgt, own, sources, ef, es, nf, ns, nc, ec, *got, pre)
    summed = row_sum(part)
    v1, v0 = swap(summed, "dom", 1), swap(summed, "dom", 0)
    return pl.pallas_call(
        functools.partial(coarse_kernel, row_nodes=row_nodes, fan=fan, rows=rows),
        out_shape=[shape((slots, width), BF)] * 2,
        in_specs=[VMEM] * 4 + [SMEM] + [HBM] * 7,
        out_specs=[HBM] * 2,
        scratch_shapes=like(own)
        + like(mf, ms, cf, cs, pf, ps)
        + [
            pltpu.VMEM((3 * row_nodes, 2 * width), BF),
            pltpu.VMEM((slots, width), BF),
            pltpu.VMEM((slots, width), BF),
            dma((7,)),
            dma((2 * slots // rows,)),
        ],
        compiler_params=params(),
        name="coarse",
    )(summed, v0, v1, first, nc, own, mf, ms, cf, cs, pf, ps)


def solution(mesh):
    parts = ("dom", "grp")
    rows = P(parts, None)
    in_specs = (rows,) * 3 + (P(parts),) * 2 + (P(parts, None, None),) + (rows,) * 4 + (P(),) * 10
    return jax.shard_map(
        per_device, mesh=mesh, in_specs=in_specs, out_specs=(rows, rows), check_vma=False
    )
```

```python
import functools

import jax
import jax.numpy as jnp
from jax import lax
from jax.experimental import pallas as pl
from jax.experimental.pallas import tpu as pltpu
from jax.sharding import PartitionSpec as P

BF = jnp.bfloat16
F32 = jnp.float32
I16 = jnp.int16
I32 = jnp.int32
HBM = pl.BlockSpec(memory_space=pltpu.HBM)
SMEM = pl.BlockSpec(memory_space=pltpu.SMEM)
VMEM = pl.BlockSpec(memory_space=pltpu.VMEM)
LANES = 128


def mm(a, b):
    return jnp.dot(a, b, preferred_element_type=F32)


def twice(weight):
    zero = jnp.zeros_like(weight)
    return jnp.concatenate(
        [jnp.concatenate([weight, zero], 1), jnp.concatenate([zero, weight], 1)], 0
    )


def centred(weight):
    weight = weight.astype(F32)
    return (weight - jnp.mean(weight, axis=1, keepdims=True)).astype(BF)


def averaging(width):
    return twice(jnp.full((width, width), 1.0 / width, BF))


def column(row):
    count = row.shape[1]
    parts = [
        jnp.broadcast_to(row[:, k : k + LANES], (LANES, LANES)).T for k in range(0, count, LANES)
    ]
    return jnp.concatenate(parts, 0).astype(I16)


def picks(col, count):
    lane = lax.broadcasted_iota(I32, (1, LANES), 1).astype(I16)
    one, zero = jnp.ones((), BF), jnp.zeros((), BF)
    return [
        jnp.where(col == jnp.broadcast_to(lane + jnp.asarray(k, I16), col.shape), one, zero)
        for k in range(0, count, LANES)
    ]


def row_picks(row, count, begin=0):
    place = (lax.broadcasted_iota(I32, (count, LANES), 0) + begin).astype(I16)
    one, zero = jnp.ones((), BF), jnp.zeros((), BF)
    parts = []
    for k in range(0, row.shape[1], LANES):
        few = jnp.broadcast_to(row[:, k : k + LANES], (16, LANES)).astype(I16)
        parts.append(jnp.where(jnp.concatenate([few] * (count // 16), 0) == place, one, zero))
    return jnp.concatenate(parts, 1)


def activated(pre):
    width = pre.shape[1] // 2
    value, tangent = pre[:, :width], pre[:, width:]
    gate = 0.5 + 0.5 * jnp.tanh(0.5 * value)
    hidden = value * gate
    slope = gate + hidden * (1.0 - gate)
    return jnp.concatenate([hidden, tangent * slope], 1)


def normed(pre, second, ones):
    width = pre.shape[1] // 2
    both = mm(activated(pre).astype(BF), second)
    value, tangent = both[:, :width], both[:, width:]
    stats = mm(jnp.concatenate([value * value, value * tangent], 1).astype(BF), ones)
    scale = lax.rsqrt(stats[:, :width] + 1e-05)
    return value * scale, scale * (tangent - value * (scale * scale * stats[:, width:]))


def fetch(pairs, sems):
    copies = [pltpu.make_async_copy(src, dst, sems.at[k]) for k, (src, dst) in enumerate(pairs)]
    for copy in copies:
        copy.start()
    return copies


def halo_kernel(nl, nt, lists, o0, o1, o2, o3, nl_v, nt_v, lists_v, sems):
    for copy in fetch([(nl, nl_v), (nt, nt_v), (lists, lists_v)], sems):
        copy.wait()
    slots = nl.shape[0]
    paired = jnp.concatenate([nl_v[...], nt_v[...]], 1)
    even = (lax.rem(lax.axis_index("dom"), 2) == 0, lax.rem(lax.axis_index("grp"), 2) == 0)
    for k, out in enumerate((o0, o1, o2, o3)):
        base = k // 2 * 2
        up = even[k // 2] if k % 2 == 0 else jnp.logical_not(even[k // 2])
        row = jnp.where(up, lists_v[0, base : base + 1, :], lists_v[0, base + 1 : base + 2, :])
        selector = jnp.concatenate(picks(column(row), slots), 1)
        out[...] = mm(selector, paired).astype(BF)


def local_kernel(nl, nt, src, tgt, ef, pre_o, nl_v, nt_v, src_v, tgt_v, ef_v, table, pre_v, sems, out_sems, *, block):
    copies = fetch([(nl, nl_v), (nt, nt_v), (ef, ef_v), (src, src_v), (tgt, tgt_v)], sems)
    for copy in copies:
        copy.wait()
    slots, width = nl.shape
    paired = jnp.concatenate([nl_v[...], nt_v[...]], 1)
    table[0:slots, :] = mm(paired, twice(ef_v[width : 2 * width, :])).astype(BF)
    table[slots:, :] = mm(paired, twice(ef_v[2 * width :, :])).astype(BF)
    stores = []
    for k, begin in enumerate(range(0, pre_o.shape[0], block)):
        at = slice(begin, begin + block)
        selector = jnp.concatenate(
            picks(column(src_v[0:1, at]), slots) + picks(column(tgt_v[0:1, at]), slots), 1
        )
        pre_v[at, :] = mm(selector, table[...])
        copy = pltpu.make_async_copy(pre_v.at[at], pre_o.at[at], out_sems.at[k])
        copy.start()
        stores.append(copy)
    for copy in stores:
        copy.wait()


def edge_kernel(nl, nt, ed, src, tgt, own, sources, ef, es, nf, ns, nc, ec, h0, h1, h2, h3, pre,
                first_o, part_o,
                nl_v, nt_v, ed_v, src_v, tgt_v, own_v, sources_v, ef_v, es_v, nf_v, ns_v,
                table, pairs, sums, pre_v, sems, pre_sems, *, block, rows):
    copies = fetch(
        list(zip(
            (ef, src, es, ed, tgt, nl, nt, nf, ns, own, sources),
            (ef_v, src_v, es_v, ed_v, tgt_v, nl_v, nt_v, nf_v, ns_v, own_v, sources_v),
        )),
        sems,
    )
    slots, width = nl.shape
    edges = ed.shape[0]
    rim = h0.shape[0]
    cuts = [slice(begin, begin + block) for begin in range(0, edges, block)]
    given_copies = fetch([(pre.at[at], pre_v.at[at]) for at in cuts], pre_sems)
    for copy in copies[:3]:
        copy.wait()
    weight = twice(ef_v[width : 2 * width, :])
    odd = (lax.rem(lax.axis_index("dom"), 2), lax.rem(lax.axis_index("grp"), 2))
    for k, got in enumerate((h0, h1, h2, h3)):
        place = k // 2 * 2 + (odd[k // 2] if k % 2 else 1 - odd[k // 2])
        at = pl.ds(pl.multiple_of(place * rim, rim), rim)
        table[at, :] = mm(got[...], weight).astype(BF)
    second = twice(centred(es_v[...]))
    ones = averaging(width)
    own_weight = ef_v[0:width, :]
    for copy in copies[3:]:
        copy.wait()
    for at, copy in zip(cuts, given_copies):
        copy.wait()
        selector = jnp.concatenate(picks(column(src_v[0:1, at] - slots), 4 * rim), 1)
        mine = ed_v[at, :]
        given = pre_v[at, :] + mm(selector, table[...])
        given = jnp.concatenate([given[:, :width] + mm(mine, own_weight), given[:, width:]], 1)
        value, tangent = normed(given, second, ones)
        pairs[at, :] = jnp.concatenate([mine.astype(F32) + value, tangent], 1).astype(BF)
    target = jnp.where(lax.broadcasted_iota(I32, (1, edges), 1) < ec[0], tgt_v[...], -1)
    owner = jnp.where(lax.broadcasted_iota(I32, (1, slots), 1) < nc[0], own_v[...], -1)
    fixed = twice(nf_v[0:width, :])
    added = twice(nf_v[width:, :])
    second = twice(centred(ns_v[...]))
    fan, owned = sources.shape
    row_nodes = owned * lax.axis_size("grp")
    for begin in range(0, slots, rows):
        sums[begin : begin + rows, :] = mm(row_picks(target, rows, begin), pairs[...]).astype(BF)
    paired = jnp.concatenate([nl_v[...], nt_v[...]], 1)
    value, tangent = normed(mm(paired, fixed) + mm(sums[...], added), second, ones)
    first = (paired.astype(F32) + jnp.concatenate([value, tangent], 1)).astype(BF)
    first_o[...] = first
    part_o[0:row_nodes, :] = mm(row_picks(owner, row_nodes), first).astype(BF)
    high = (sources_v[...] // 256).astype(F32).astype(BF)
    low = lax.rem(sources_v[...], 256).astype(F32).astype(BF)
    lane = lax.broadcasted_iota(I32, (owned, 2 * width), 1)
    spot = lax.broadcasted_iota(I32, (owned, 2 * width), 0) + lax.axis_index("grp") * owned
    for k in range((part_o.shape[0] - row_nodes) // (2 * fan)):
        place = jnp.where(lane + k * 2 * width == spot, jnp.ones((), F32), jnp.zeros((), F32)).astype(BF)
        base = row_nodes + k * 2 * fan
        part_o[base : base + 2 * fan, :] = jnp.concatenate([mm(high, place), mm(low, place)], 0).astype(BF)


def coarse_kernel(summed, v0, v1, first, nc, own, mf, ms, cf, cs, pf, ps,
                  node_o, tangent_o,
                  own_v, mf_v, ms_v, cf_v, cs_v, pf_v, ps_v,
                  table, node_v, tangent_v, sems, out_sems, *, row_nodes, fan, rows):
    copies = fetch(
        list(zip(
            (mf, ms, cf, cs, pf, ps, own),
            (mf_v, ms_v, cf_v, cs_v, pf_v, ps_v, own_v),
        )),
        sems,
    )
    for copy in copies:
        copy.wait()
    slots, width = node_o.shape
    ones = averaging(width)
    mine = summed[0:row_nodes, :]
    weight = twice(mf_v[0:width, :])
    table[row_nodes : 2 * row_nodes, :] = mm(mine, weight).astype(BF)
    odd = lax.rem(lax.axis_index("dom"), 2)
    for k, got in enumerate((v0, v1)):
        place = 2 * odd if k else 2 - 2 * odd
        at = pl.ds(pl.multiple_of(place * row_nodes, row_nodes), row_nodes)
        table[at, :] = mm(got[0:row_nodes, :], weight).astype(BF)
    received = mm(mine, twice(mf_v[width:, :]))
    sums = []
    for begin in range(0, row_nodes, LANES):
        chunk, lanes = divmod(begin, 2 * width)
        base = row_nodes + chunk * 2 * fan
        spots = summed[base : base + 2 * fan, lanes : lanes + LANES].astype(F32)
        spots = (spots[0:fan, :] * 256.0 + spots[fan:, :]).astype(I32)
        got = received[begin : begin + LANES, :]
        selector = jnp.concatenate([column(spots[j : j + 1, :]) for j in range(fan)], 0)
        pre = mm(jnp.concatenate(picks(selector, 3 * row_nodes), 1), table[...])
        hidden = activated(pre + jnp.concatenate([got] * fan, 0))
        sums.append(sum(hidden[j * LANES : (j + 1) * LANES, :] for j in range(fan)))
    hidden = jnp.concatenate(sums, 0)
    weight = twice(ms_v[...])
    large = hidden.astype(BF)
    message = (mm(large, weight) + mm((hidden - large.astype(F32)).astype(BF), weight)).astype(BF)
    pre = mm(mine, twice(cf_v[0:width, :])) + mm(message, twice(cf_v[width:, :]))
    value, tangent = normed(pre, twice(centred(cs_v[...])), ones)
    updated = jnp.concatenate([value, tangent], 1).astype(BF)
    brought = mm(updated, twice(pf_v[width:, :])).astype(BF)
    fixed = twice(pf_v[0:width, :])
    second = twice(centred(ps_v[...]))
    stores = []
    for k, begin in enumerate(range(0, slots, rows)):
        at = slice(begin, begin + rows)
        selector = jnp.concatenate(picks(column(own_v[:, at]), row_nodes), 1)
        block = first[at, :]
        value, tangent = normed(mm(block, fixed) + mm(selector, brought), second, ones)
        valid = lax.broadcasted_iota(I32, (rows, 1), 0) + begin < nc[0]
        node_v[at, :] = jnp.where(valid, block[:, :width].astype(F32) + value, 0.0).astype(BF)
        tangent_v[at, :] = jnp.where(valid, block[:, width:].astype(F32) + tangent, 0.0).astype(BF)
        for i, (held, out) in enumerate(((node_v, node_o), (tangent_v, tangent_o))):
            copy = pltpu.make_async_copy(held.at[at], out.at[at], out_sems.at[2 * k + i])
            copy.start()
            stores.append(copy)
    for copy in stores:
        copy.wait()


def like(*arrays):
    return [pltpu.VMEM(a.shape, a.dtype) for a in arrays]


def params(mib=40):
    return pltpu.CompilerParams(vmem_limit_bytes=int(mib * 2**20))


def swap(x, axis, first):
    pairs = []
    for i in range(first, lax.axis_size(axis) - 1, 2):
        pairs += [(i, i + 1), (i + 1, i)]
    return lax.ppermute(x, axis, pairs)


def row_sum(x):
    size = lax.axis_size("grp")
    total = x.astype(F32)
    for by in range(1, size):
        if size & (size - 1) == 0:
            pairs = [(i, i ^ by) for i in range(size)]
        else:
            pairs = [(i, (i + by) % size) for i in range(size)]
        total = total + lax.ppermute(x, "grp", pairs).astype(F32)
    return total.astype(BF)


def per_device(nl, nt, ed, nc, ec, lists, src, tgt, own, sources, ef, es, nf, ns, mf, ms, cf, cs, pf, ps):
    slots, width = nl.shape
    edges = ed.shape[0]
    rim = lists.shape[2]
    owned, fan = sources.shape
    sources = sources.T
    row_nodes = owned * lax.axis_size("grp")
    extra = 2 * fan * (-(-row_nodes // (2 * width)))
    rows, block, cut = min(slots, 512), min(edges, 1024), min(edges, 512)
    shape = jax.ShapeDtypeStruct
    dma = pltpu.SemaphoreType.DMA
    sent = pl.pallas_call(
        halo_kernel,
        out_shape=[shape((rim, 2 * width), BF)] * 4,
        in_specs=[HBM] * 3,
        out_specs=[VMEM] * 4,
        scratch_shapes=like(nl, nt, lists) + [dma((3,))],
        compiler_params=params(60),
        name="halo_rows",
    )(nl, nt, lists)
    got = [swap(sent[k], ("dom", "grp")[k // 2], k % 2) for k in range(4)]
    pre = pl.pallas_call(
        functools.partial(local_kernel, block=cut),
        out_shape=shape((edges, 2 * width), F32),
        in_specs=[HBM] * 5,
        out_specs=HBM,
        scratch_shapes=like(nl, nt, src, tgt, ef)
        + [
            pltpu.VMEM((2 * slots, 2 * width), BF),
            pltpu.VMEM((edges, 2 * width), F32),
            dma((5,)),
            dma((edges // cut,)),
        ],
        compiler_params=params(59),
        cost_estimate=pl.CostEstimate(
            flops=8 * edges * slots * width, bytes_accessed=8 * edges * width, transcendentals=0
        ),
        name="local",
    )(nl, nt, src, tgt, ef)
    first, part = pl.pallas_call(
        functools.partial(edge_kernel, block=block, rows=rows),
        out_shape=[shape((slots, 2 * width), BF), shape((row_nodes + extra, 2 * width), BF)],
        in_specs=[HBM] * 11 + [SMEM] * 2 + [VMEM] * 4 + [HBM],
        out_specs=[VMEM] * 2,
        scratch_shapes=like(nl, nt, ed, src, tgt, own, sources)
        + like(ef, es, nf, ns)
        + [pltpu.VMEM((4 * rim, 2 * width), BF), pltpu.VMEM((edges, 2 * width), BF), pltpu.VMEM((slots, 2 * width), BF)]
        + [pltpu.VMEM((edges, 2 * width), F32), dma((11,)), dma((edges // block,))],
        compiler_params=params(51),
        name="edges",
    )(nl, nt, ed, src, tgt, own, sources, ef, es, nf, ns, nc, ec, *got, pre)
    summed = row_sum(part)
    v1, v0 = swap(summed, "dom", 1), swap(summed, "dom", 0)
    return pl.pallas_call(
        functools.partial(coarse_kernel, row_nodes=row_nodes, fan=fan, rows=slots),
        out_shape=[shape((slots, width), BF)] * 2,
        in_specs=[VMEM] * 4 + [SMEM] + [HBM] * 7,
        out_specs=[HBM] * 2,
        scratch_shapes=like(own)
        + like(mf, ms, cf, cs, pf, ps)
        + [
            pltpu.VMEM((3 * row_nodes, 2 * width), BF),
            pltpu.VMEM((slots, width), BF),
            pltpu.VMEM((slots, width), BF),
            dma((7,)),
            dma((2,)),
        ],
        compiler_params=params(),
        name="coarse",
    )(summed, v0, v1, first, nc, own, mf, ms, cf, cs, pf, ps)


def solution(mesh):
    parts = ("dom", "grp")
    rows = P(parts, None)
    in_specs = (rows,) * 3 + (P(parts),) * 2 + (P(parts, None, None),) + (rows,) * 4 + (P(),) * 10
    return jax.shard_map(
        per_device, mesh=mesh, in_specs=in_specs, out_specs=(rows, rows), check_vma=False
    )
```

```python
import functools

import jax
import jax.numpy as jnp
from jax import lax
from jax.experimental import pallas as pl
from jax.experimental.pallas import tpu as pltpu
from jax.sharding import PartitionSpec as P

BF = jnp.bfloat16
F32 = jnp.float32
I16 = jnp.int16
I32 = jnp.int32
HBM = pl.BlockSpec(memory_space=pltpu.HBM)
SMEM = pl.BlockSpec(memory_space=pltpu.SMEM)
VMEM = pl.BlockSpec(memory_space=pltpu.VMEM)
LANES = 128


def mm(a, b):
    return jnp.dot(a, b, preferred_element_type=F32)


def twice(weight):
    zero = jnp.zeros_like(weight)
    return jnp.concatenate(
        [jnp.concatenate([weight, zero], 1), jnp.concatenate([zero, weight], 1)], 0
    )


def centred(weight):
    weight = weight.astype(F32)
    return (weight - jnp.mean(weight, axis=1, keepdims=True)).astype(BF)


def averaging(width):
    return twice(jnp.full((width, width), 1.0 / width, BF))


def column(row):
    count = row.shape[1]
    parts = [
        jnp.broadcast_to(row[:, k : k + LANES], (LANES, LANES)).T for k in range(0, count, LANES)
    ]
    return jnp.concatenate(parts, 0).astype(I16)


def picks(col, count):
    lane = lax.broadcasted_iota(I32, (1, LANES), 1).astype(I16)
    one, zero = jnp.ones((), BF), jnp.zeros((), BF)
    return [
        jnp.where(col == jnp.broadcast_to(lane + jnp.asarray(k, I16), col.shape), one, zero)
        for k in range(0, count, LANES)
    ]


def row_picks(row, count, begin=0):
    place = (lax.broadcasted_iota(I32, (count, LANES), 0) + begin).astype(I16)
    one, zero = jnp.ones((), BF), jnp.zeros((), BF)
    parts = []
    for k in range(0, row.shape[1], LANES):
        few = jnp.broadcast_to(row[:, k : k + LANES], (16, LANES)).astype(I16)
        parts.append(jnp.where(jnp.concatenate([few] * (count // 16), 0) == place, one, zero))
    return jnp.concatenate(parts, 1)


def activated(pre):
    width = pre.shape[1] // 2
    value, tangent = pre[:, :width], pre[:, width:]
    gate = 0.5 + 0.5 * jnp.tanh(0.5 * value)
    hidden = value * gate
    slope = gate + hidden * (1.0 - gate)
    return jnp.concatenate([hidden, tangent * slope], 1)


def normed(pre, second, ones):
    width = pre.shape[1] // 2
    both = mm(activated(pre).astype(BF), second)
    value, tangent = both[:, :width], both[:, width:]
    stats = mm(jnp.concatenate([value * value, value * tangent], 1).astype(BF), ones)
    scale = lax.rsqrt(stats[:, :width] + 1e-05)
    return value * scale, scale * (tangent - value * (scale * scale * stats[:, width:]))


def fetch(pairs, sems):
    copies = [pltpu.make_async_copy(src, dst, sems.at[k]) for k, (src, dst) in enumerate(pairs)]
    for copy in copies:
        copy.start()
    return copies


def halo_kernel(nl, nt, lists, o0, o1, o2, o3, nl_v, nt_v, lists_v, sent_v, sems, out_sems):
    for copy in fetch([(lists, lists_v), (nl, nl_v), (nt, nt_v)], sems):
        copy.wait()
    slots = nl.shape[0]
    rim = o0.shape[0]
    paired = jnp.concatenate([nl_v[...], nt_v[...]], 1)
    even = (lax.rem(lax.axis_index("dom"), 2) == 0, lax.rem(lax.axis_index("grp"), 2) == 0)
    stores = []
    for k, out in enumerate((o0, o1, o2, o3)):
        base = k // 2 * 2
        up = even[k // 2] if k % 2 == 0 else jnp.logical_not(even[k // 2])
        row = jnp.where(up, lists_v[0, base : base + 1, :], lists_v[0, base + 1 : base + 2, :])
        selector = jnp.concatenate(picks(column(row), slots), 1)
        at = slice(k * rim, (k + 1) * rim)
        sent_v[at, :] = mm(selector, paired).astype(BF)
        copy = pltpu.make_async_copy(sent_v.at[at], out, out_sems.at[k])
        copy.start()
        stores.append(copy)
    for copy in stores:
        copy.wait()


def local_kernel(nl, nt, src, tgt, ef, pre_o, table, *, block):
    slots, width = nl.shape
    paired = jnp.concatenate([nl[...], nt[...]], 1)
    table[0:slots, :] = mm(paired, twice(ef[width : 2 * width, :])).astype(BF)
    table[slots:, :] = mm(paired, twice(ef[2 * width :, :])).astype(BF)
    for begin in range(0, pre_o.shape[0], block):
        at = slice(begin, begin + block)
        selector = jnp.concatenate(
            picks(column(src[0:1, at]), slots) + picks(column(tgt[0:1, at]), slots), 1
        )
        pre_o[at, :] = mm(selector, table[...])


def edge_kernel(nl_v, nt_v, ed_v, src_v, tgt_v, own_v, sources_v, ef_v, es_v, nf_v, ns_v, nc, ec,
                h0, h1, h2, h3, pre, first_o, part_o, table, pairs, sums, *, block, rows):
    slots, width = nl_v.shape
    edges = ed_v.shape[0]
    rim = h0.shape[0]
    weight = twice(ef_v[width : 2 * width, :])
    odd = (lax.rem(lax.axis_index("dom"), 2), lax.rem(lax.axis_index("grp"), 2))
    for k, got in enumerate((h0, h1, h2, h3)):
        place = k // 2 * 2 + (odd[k // 2] if k % 2 else 1 - odd[k // 2])
        at = pl.ds(pl.multiple_of(place * rim, rim), rim)
        table[at, :] = mm(got[...], weight).astype(BF)
    second = twice(centred(es_v[...]))
    ones = averaging(width)
    own_weight = ef_v[0:width, :]
    for begin in range(0, edges, block):
        at = slice(begin, begin + block)
        selector = jnp.concatenate(picks(column(src_v[0:1, at] - slots), 4 * rim), 1)
        mine = ed_v[at, :]
        given = pre[at, :] + mm(selector, table[...])
        given = jnp.concatenate([given[:, :width] + mm(mine, own_weight), given[:, width:]], 1)
        value, tangent = normed(given, second, ones)
        pairs[at, :] = jnp.concatenate([mine.astype(F32) + value, tangent], 1).astype(BF)
    target = jnp.where(lax.broadcasted_iota(I32, (1, edges), 1) < ec[0], tgt_v[...], -1)
    owner = jnp.where(lax.broadcasted_iota(I32, (1, slots), 1) < nc[0], own_v[...], -1)
    fixed = twice(nf_v[0:width, :])
    added = twice(nf_v[width:, :])
    second = twice(centred(ns_v[...]))
    fan, owned = sources_v.shape
    row_nodes = owned * lax.axis_size("grp")
    for begin in range(0, slots, rows):
        sums[begin : begin + rows, :] = mm(row_picks(target, rows, begin), pairs[...]).astype(BF)
    paired = jnp.concatenate([nl_v[...], nt_v[...]], 1)
    value, tangent = normed(mm(paired, fixed) + mm(sums[...], added), second, ones)
    first = (paired.astype(F32) + jnp.concatenate([value, tangent], 1)).astype(BF)
    first_o[...] = first
    part_o[0:row_nodes, :] = mm(row_picks(owner, row_nodes), first).astype(BF)
    high = (sources_v[...] // 256).astype(F32).astype(BF)
    low = lax.rem(sources_v[...], 256).astype(F32).astype(BF)
    lane = lax.broadcasted_iota(I32, (owned, 2 * width), 1)
    spot = lax.broadcasted_iota(I32, (owned, 2 * width), 0) + lax.axis_index("grp") * owned
    for k in range((part_o.shape[0] - row_nodes) // (2 * fan)):
        place = jnp.where(lane + k * 2 * width == spot, jnp.ones((), F32), jnp.zeros((), F32)).astype(BF)
        base = row_nodes + k * 2 * fan
        part_o[base : base + 2 * fan, :] = jnp.concatenate([mm(high, place), mm(low, place)], 0).astype(BF)


def prepare_kernel(first, own, mf, ms, cf, cs, pf, ps, weights_o, fixed_o, owner_o):
    width = mf.shape[1]
    size = 2 * width
    stack = (
        twice(mf[0:width, :]),
        twice(mf[width:, :]),
        twice(ms[...]),
        twice(cf[0:width, :]),
        twice(cf[width:, :]),
        twice(centred(cs[...])),
        twice(pf[width:, :]),
        twice(centred(ps[...])),
    )
    for k, weight in enumerate(stack):
        weights_o[k * size : (k + 1) * size, :] = weight
    fixed_o[...] = mm(first[...], twice(pf[0:width, :]))
    owner_o[...] = jnp.concatenate(picks(column(own[...]), owner_o.shape[1]), 1)


def own_row_kernel(summed, weights, given_o, outer_o, mine_o, *, fan):
    row_nodes, size = mine_o.shape
    mine = summed[0:row_nodes, :]
    table = mm(mine, weights[0:size, :]).astype(BF)
    received = mm(mine, weights[size : 2 * size, :])
    for begin in range(0, row_nodes, LANES):
        chunk, lanes = divmod(begin, size)
        base = row_nodes + chunk * 2 * fan
        spots = summed[base : base + 2 * fan, lanes : lanes + LANES].astype(F32)
        spots = (spots[0:fan, :] * 256.0 + spots[fan:, :]).astype(I32)
        spots = jnp.concatenate([column(spots[j : j + 1, :]) for j in range(fan)], 0)
        blocks = picks(spots, 3 * row_nodes)
        few = row_nodes // LANES
        at = slice(begin * fan, (begin + LANES) * fan)
        got = received[begin : begin + LANES, :]
        given_o[at, :] = mm(jnp.concatenate(blocks[few : 2 * few], 1), table) + jnp.concatenate([got] * fan, 0)
        outer_o[at, :] = jnp.concatenate(blocks[:few] + blocks[2 * few :], 1)
    mine_o[...] = mm(mine, weights[3 * size : 4 * size, :])


def coarse_kernel(v0, v1, given, outer, mine, weights, fixed, owner, first, nc,
                  node_o, tangent_o, table, node_v, tangent_v, out_sems, *, fan):
    slots, width = node_o.shape
    row_nodes, size = mine.shape
    held = [weights[k * size : (k + 1) * size, :] for k in range(8)]
    ones = averaging(width)
    odd = lax.rem(lax.axis_index("dom"), 2)
    for k, got in enumerate((v0, v1)):
        place = odd if k else 1 - odd
        at = pl.ds(pl.multiple_of(place * row_nodes, row_nodes), row_nodes)
        table[at, :] = mm(got[0:row_nodes, :], held[0]).astype(BF)
    hidden = activated(given[...] + mm(outer[...], table[...]))
    sums = []
    for begin in range(0, row_nodes, LANES):
        part = [hidden[begin * fan + j * LANES : begin * fan + (j + 1) * LANES, :] for j in range(fan)]
        sums.append(sum(part))
    hidden = jnp.concatenate(sums, 0)
    large = hidden.astype(BF)
    message = mm(large, held[2]) + mm((hidden - large.astype(F32)).astype(BF), held[2])
    value, tangent = normed(mine[...] + mm(message.astype(BF), held[4]), held[5], ones)
    updated = jnp.concatenate([value, tangent], 1).astype(BF)
    brought = mm(updated, held[6]).astype(BF)
    value, tangent = normed(fixed[...] + mm(owner[...], brought), held[7], ones)
    base = first[...].astype(F32)
    valid = lax.broadcasted_iota(I32, (slots, 1), 0) < nc[0]
    node_v[...] = jnp.where(valid, base[:, :width] + value, 0.0).astype(BF)
    tangent_v[...] = jnp.where(valid, base[:, width:] + tangent, 0.0).astype(BF)
    for copy in fetch([(node_v, node_o), (tangent_v, tangent_o)], out_sems):
        copy.wait()


def like(*arrays):
    return [pltpu.VMEM(a.shape, a.dtype) for a in arrays]


def params(mib=40):
    return pltpu.CompilerParams(vmem_limit_bytes=int(mib * 2**20))


def swap(x, axis, first):
    pairs = []
    for i in range(first, lax.axis_size(axis) - 1, 2):
        pairs += [(i, i + 1), (i + 1, i)]
    return lax.ppermute(x, axis, pairs)


def row_sum(x):
    size = lax.axis_size("grp")
    total = x.astype(F32)
    for by in range(1, size):
        if size & (size - 1) == 0:
            pairs = [(i, i ^ by) for i in range(size)]
        else:
            pairs = [(i, (i + by) % size) for i in range(size)]
        total = total + lax.ppermute(x, "grp", pairs).astype(F32)
    return total.astype(BF)


def per_device(nl, nt, ed, nc, ec, lists, src, tgt, own, sources, ef, es, nf, ns, mf, ms, cf, cs, pf, ps):
    slots, width = nl.shape
    edges = ed.shape[0]
    rim = lists.shape[2]
    owned, fan = sources.shape
    sources = sources.T
    row_nodes = owned * lax.axis_size("grp")
    extra = 2 * fan * (-(-row_nodes // (2 * width)))
    rows, block, cut = min(slots, 512), min(edges, 1024), min(edges, 512)
    shape = jax.ShapeDtypeStruct
    dma = pltpu.SemaphoreType.DMA
    sent = pl.pallas_call(
        halo_kernel,
        out_shape=[shape((rim, 2 * width), BF)] * 4,
        in_specs=[HBM] * 3,
        out_specs=[HBM] * 4,
        scratch_shapes=like(nl, nt, lists) + [pltpu.VMEM((4 * rim, 2 * width), BF), dma((3,)), dma((4,))],
        compiler_params=params(60),
        cost_estimate=pl.CostEstimate(flops=8 * edges * slots * width, bytes_accessed=4 * slots * width, transcendentals=0),
        name="halo_rows",
    )(nl, nt, lists)
    got = [swap(sent[k], ("dom", "grp")[k // 2], k % 2) for k in range(4)]
    pre = pl.pallas_call(
        functools.partial(local_kernel, block=cut),
        out_shape=shape((edges, 2 * width), F32),
        in_specs=[VMEM] * 5,
        out_specs=VMEM,
        scratch_shapes=[pltpu.VMEM((2 * slots, 2 * width), BF)],
        compiler_params=params(),
        cost_estimate=pl.CostEstimate(
            flops=8 * edges * slots * width, bytes_accessed=8 * edges * width, transcendentals=0
        ),
        name="local",
    )(nl, nt, src, tgt, ef)
    first, part = pl.pallas_call(
        functools.partial(edge_kernel, block=block, rows=rows),
        out_shape=[shape((slots, 2 * width), BF), shape((row_nodes + extra, 2 * width), BF)],
        in_specs=[VMEM] * 11 + [SMEM] * 2 + [VMEM] * 5,
        out_specs=[VMEM] * 2,
        scratch_shapes=[
            pltpu.VMEM((4 * rim, 2 * width), BF),
            pltpu.VMEM((edges, 2 * width), BF),
            pltpu.VMEM((slots, 2 * width), BF),
        ],
        compiler_params=params(),
        name="edges",
    )(nl, nt, ed, src, tgt, own, sources, ef, es, nf, ns, nc, ec, *got, pre)
    weights, fixed, owner = pl.pallas_call(
        prepare_kernel,
        out_shape=[
            shape((16 * width, 2 * width), BF),
            shape((slots, 2 * width), F32),
            shape((slots, row_nodes), BF),
        ],
        in_specs=[VMEM] * 8,
        out_specs=[VMEM] * 3,
        compiler_params=params(),
        cost_estimate=pl.CostEstimate(
            flops=8 * slots * width * width, bytes_accessed=slots * width * 32, transcendentals=0
        ),
        name="prepare",
    )(first, own, mf, ms, cf, cs, pf, ps)
    summed = row_sum(part)
    v1, v0 = swap(summed, "dom", 1), swap(summed, "dom", 0)
    given, outer, mine = pl.pallas_call(
        functools.partial(own_row_kernel, fan=fan),
        out_shape=[
            shape((fan * row_nodes, 2 * width), F32),
            shape((fan * row_nodes, 2 * row_nodes), BF),
            shape((row_nodes, 2 * width), F32),
        ],
        in_specs=[VMEM] * 2,
        out_specs=[VMEM] * 3,
        compiler_params=params(),
        cost_estimate=pl.CostEstimate(
            flops=4 * fan * row_nodes * row_nodes * width,
            bytes_accessed=slots * width * 32,
            transcendentals=0,
        ),
        name="own_row",
    )(summed, weights)
    return pl.pallas_call(
        functools.partial(coarse_kernel, fan=fan),
        out_shape=[shape((slots, width), BF)] * 2,
        in_specs=[VMEM] * 9 + [SMEM],
        out_specs=[HBM] * 2,
        scratch_shapes=[
            pltpu.VMEM((2 * row_nodes, 2 * width), BF),
            pltpu.VMEM((slots, width), BF),
            pltpu.VMEM((slots, width), BF),
            dma((2,)),
        ],
        compiler_params=params(),
        name="coarse",
    )(v0, v1, given, outer, mine, weights, fixed, owner, first, nc)


def solution(mesh):
    parts = ("dom", "grp")
    rows = P(parts, None)
    in_specs = (rows,) * 3 + (P(parts),) * 2 + (P(parts, None, None),) + (rows,) * 4 + (P(),) * 10
    return jax.shard_map(
        per_device, mesh=mesh, in_specs=in_specs, out_specs=(rows, rows), check_vma=False
    )
```

```python
import functools

import jax
import jax.numpy as jnp
from jax import lax
from jax.experimental import pallas as pl
from jax.experimental.pallas import tpu as pltpu
from jax.sharding import PartitionSpec as P

BF = jnp.bfloat16
F32 = jnp.float32
I16 = jnp.int16
I32 = jnp.int32
HBM = pl.BlockSpec(memory_space=pltpu.HBM)
SMEM = pl.BlockSpec(memory_space=pltpu.SMEM)
VMEM = pl.BlockSpec(memory_space=pltpu.VMEM)
LANES = 128


def mm(a, b):
    return jnp.dot(a, b, preferred_element_type=F32)


def twice(weight):
    zero = jnp.zeros_like(weight)
    return jnp.concatenate(
        [jnp.concatenate([weight, zero], 1), jnp.concatenate([zero, weight], 1)], 0
    )


def centred(weight):
    weight = weight.astype(F32)
    return (weight - jnp.mean(weight, axis=1, keepdims=True)).astype(BF)


def averaging(width):
    return twice(jnp.full((width, width), 1.0 / width, BF))


def column(row):
    count = row.shape[1]
    parts = [
        jnp.broadcast_to(row[:, k : k + LANES], (LANES, LANES)).T for k in range(0, count, LANES)
    ]
    return jnp.concatenate(parts, 0).astype(I16)


def picks(col, count):
    lane = lax.broadcasted_iota(I32, (1, LANES), 1).astype(I16)
    one, zero = jnp.ones((), BF), jnp.zeros((), BF)
    return [
        jnp.where(col == jnp.broadcast_to(lane + jnp.asarray(k, I16), col.shape), one, zero)
        for k in range(0, count, LANES)
    ]


def row_picks(row, count, begin=0):
    place = (lax.broadcasted_iota(I32, (count, LANES), 0) + begin).astype(I16)
    one, zero = jnp.ones((), BF), jnp.zeros((), BF)
    parts = []
    for k in range(0, row.shape[1], LANES):
        few = jnp.broadcast_to(row[:, k : k + LANES], (16, LANES)).astype(I16)
        parts.append(jnp.where(jnp.concatenate([few] * (count // 16), 0) == place, one, zero))
    return jnp.concatenate(parts, 1)


def activated(pre):
    width = pre.shape[1] // 2
    value, tangent = pre[:, :width], pre[:, width:]
    gate = 0.5 + 0.5 * jnp.tanh(0.5 * value)
    hidden = value * gate
    slope = gate + hidden * (1.0 - gate)
    return jnp.concatenate([hidden, tangent * slope], 1)


def normed(pre, second, ones):
    width = pre.shape[1] // 2
    both = mm(activated(pre).astype(BF), second)
    value, tangent = both[:, :width], both[:, width:]
    stats = mm(jnp.concatenate([value * value, value * tangent], 1).astype(BF), ones)
    scale = lax.rsqrt(stats[:, :width] + 1e-05)
    return value * scale, scale * (tangent - value * (scale * scale * stats[:, width:]))


def fetch(pairs, sems):
    copies = [pltpu.make_async_copy(src, dst, sems.at[k]) for k, (src, dst) in enumerate(pairs)]
    for copy in copies:
        copy.start()
    return copies


def halo_kernel(nl, nt, lists, o0, o1, o2, o3, nl_v, nt_v, lists_v, sems):
    for copy in fetch([(lists, lists_v), (nl, nl_v), (nt, nt_v)], sems):
        copy.wait()
    slots = nl.shape[0]
    paired = jnp.concatenate([nl_v[...], nt_v[...]], 1)
    even = (lax.rem(lax.axis_index("dom"), 2) == 0, lax.rem(lax.axis_index("grp"), 2) == 0)
    for k, out in enumerate((o0, o1, o2, o3)):
        base = k // 2 * 2
        up = even[k // 2] if k % 2 == 0 else jnp.logical_not(even[k // 2])
        row = jnp.where(up, lists_v[0, base : base + 1, :], lists_v[0, base + 1 : base + 2, :])
        selector = jnp.concatenate(picks(column(row), slots), 1)
        out[...] = mm(selector, paired).astype(BF)


def local_kernel(nl, nt, src, tgt, ef, pre_o, table, *, block):
    slots, width = nl.shape
    paired = jnp.concatenate([nl[...], nt[...]], 1)
    table[0:slots, :] = mm(paired, twice(ef[width : 2 * width, :])).astype(BF)
    table[slots:, :] = mm(paired, twice(ef[2 * width :, :])).astype(BF)
    for begin in range(0, pre_o.shape[0], block):
        at = slice(begin, begin + block)
        selector = jnp.concatenate(
            picks(column(src[0:1, at]), slots) + picks(column(tgt[0:1, at]), slots), 1
        )
        pre_o[at, :] = mm(selector, table[...])


def edge_kernel(nl_v, nt_v, ed_v, src_v, tgt_v, own_v, sources_v, ef_v, es_v, nf_v, ns_v, nc, ec,
                h0, h1, h2, h3, pre, first_o, part_o, table, pairs, sums, *, block, rows):
    slots, width = nl_v.shape
    edges = ed_v.shape[0]
    rim = h0.shape[0]
    weight = twice(ef_v[width : 2 * width, :])
    odd = (lax.rem(lax.axis_index("dom"), 2), lax.rem(lax.axis_index("grp"), 2))
    for k, got in enumerate((h0, h1, h2, h3)):
        place = k // 2 * 2 + (odd[k // 2] if k % 2 else 1 - odd[k // 2])
        at = pl.ds(pl.multiple_of(place * rim, rim), rim)
        table[at, :] = mm(got[...], weight).astype(BF)
    second = twice(centred(es_v[...]))
    ones = averaging(width)
    own_weight = ef_v[0:width, :]
    for begin in range(0, edges, block):
        at = slice(begin, begin + block)
        selector = jnp.concatenate(picks(column(src_v[0:1, at] - slots), 4 * rim), 1)
        mine = ed_v[at, :]
        given = pre[at, :] + mm(selector, table[...])
        given = jnp.concatenate([given[:, :width] + mm(mine, own_weight), given[:, width:]], 1)
        value, tangent = normed(given, second, ones)
        pairs[at, :] = jnp.concatenate([mine.astype(F32) + value, tangent], 1).astype(BF)
    target = jnp.where(lax.broadcasted_iota(I32, (1, edges), 1) < ec[0], tgt_v[...], -1)
    owner = jnp.where(lax.broadcasted_iota(I32, (1, slots), 1) < nc[0], own_v[...], -1)
    fixed = twice(nf_v[0:width, :])
    added = twice(nf_v[width:, :])
    second = twice(centred(ns_v[...]))
    fan, owned = sources_v.shape
    row_nodes = owned * lax.axis_size("grp")
    for begin in range(0, slots, rows):
        sums[begin : begin + rows, :] = mm(row_picks(target, rows, begin), pairs[...]).astype(BF)
    paired = jnp.concatenate([nl_v[...], nt_v[...]], 1)
    value, tangent = normed(mm(paired, fixed) + mm(sums[...], added), second, ones)
    first = (paired.astype(F32) + jnp.concatenate([value, tangent], 1)).astype(BF)
    first_o[...] = first
    part_o[0:row_nodes, :] = mm(row_picks(owner, row_nodes), first).astype(BF)
    high = (sources_v[...] // 256).astype(F32).astype(BF)
    low = lax.rem(sources_v[...], 256).astype(F32).astype(BF)
    lane = lax.broadcasted_iota(I32, (owned, 2 * width), 1)
    spot = lax.broadcasted_iota(I32, (owned, 2 * width), 0) + lax.axis_index("grp") * owned
    for k in range((part_o.shape[0] - row_nodes) // (2 * fan)):
        place = jnp.where(lane + k * 2 * width == spot, jnp.ones((), F32), jnp.zeros((), F32)).astype(BF)
        base = row_nodes + k * 2 * fan
        part_o[base : base + 2 * fan, :] = jnp.concatenate([mm(high, place), mm(low, place)], 0).astype(BF)


def prepare_kernel(first, own, mf, ms, cf, cs, pf, ps, weights_o, fixed_o, owner_o):
    width = mf.shape[1]
    size = 2 * width
    stack = (
        twice(mf[0:width, :]),
        twice(mf[width:, :]),
        twice(mm(ms[...], cf[width:, :]).astype(BF)),
        twice(cf[0:width, :]),
        twice(centred(cs[...])),
        twice(pf[width:, :]),
        twice(centred(ps[...])),
    )
    for k, weight in enumerate(stack):
        weights_o[k * size : (k + 1) * size, :] = weight
    fixed_o[...] = mm(first[...], twice(pf[0:width, :]))
    owner_o[...] = jnp.concatenate(picks(column(own[...]), owner_o.shape[1]), 1)


def own_row_kernel(summed, weights, given_o, outer_o, mine_o, *, fan):
    row_nodes, size = mine_o.shape
    mine = summed[0:row_nodes, :]
    table = mm(mine, weights[0:size, :]).astype(BF)
    received = mm(mine, weights[size : 2 * size, :])
    for begin in range(0, row_nodes, LANES):
        chunk, lanes = divmod(begin, size)
        base = row_nodes + chunk * 2 * fan
        spots = summed[base : base + 2 * fan, lanes : lanes + LANES].astype(F32)
        spots = (spots[0:fan, :] * 256.0 + spots[fan:, :]).astype(I32)
        spots = jnp.concatenate([column(spots[j : j + 1, :]) for j in range(fan)], 0)
        blocks = picks(spots, 3 * row_nodes)
        few = row_nodes // LANES
        at = slice(begin * fan, (begin + LANES) * fan)
        got = received[begin : begin + LANES, :]
        given_o[at, :] = mm(jnp.concatenate(blocks[few : 2 * few], 1), table) + jnp.concatenate([got] * fan, 0)
        outer_o[at, :] = jnp.concatenate(blocks[:few] + blocks[2 * few :], 1)
    mine_o[...] = mm(mine, weights[3 * size : 4 * size, :])


def coarse_kernel(v0, v1, given, outer, mine, weights, fixed, owner, first, nc,
                  node_o, tangent_o, table, node_v, tangent_v, out_sems, *, fan):
    slots, width = node_o.shape
    row_nodes, size = mine.shape
    held = [weights[k * size : (k + 1) * size, :] for k in range(7)]
    ones = averaging(width)
    odd = lax.rem(lax.axis_index("dom"), 2)
    for k, got in enumerate((v0, v1)):
        place = odd if k else 1 - odd
        at = pl.ds(pl.multiple_of(place * row_nodes, row_nodes), row_nodes)
        table[at, :] = mm(got[0:row_nodes, :], held[0]).astype(BF)
    hidden = activated(given[...] + mm(outer[...], table[...]))
    sums = []
    for begin in range(0, row_nodes, LANES):
        part = [hidden[begin * fan + j * LANES : begin * fan + (j + 1) * LANES, :] for j in range(fan)]
        sums.append(sum(part))
    hidden = jnp.concatenate(sums, 0)
    large = hidden.astype(BF)
    small = (hidden - large.astype(F32)).astype(BF)
    value, tangent = normed(mine[...] + mm(large, held[2]) + mm(small, held[2]), held[4], ones)
    updated = jnp.concatenate([value, tangent], 1).astype(BF)
    brought = mm(updated, held[5]).astype(BF)
    value, tangent = normed(fixed[...] + mm(owner[...], brought), held[6], ones)
    base = first[...].astype(F32)
    valid = lax.broadcasted_iota(I32, (slots, 1), 0) < nc[0]
    node_v[...] = jnp.where(valid, base[:, :width] + value, 0.0).astype(BF)
    tangent_v[...] = jnp.where(valid, base[:, width:] + tangent, 0.0).astype(BF)
    for copy in fetch([(node_v, node_o), (tangent_v, tangent_o)], out_sems):
        copy.wait()


def like(*arrays):
    return [pltpu.VMEM(a.shape, a.dtype) for a in arrays]


def params(mib=40):
    return pltpu.CompilerParams(vmem_limit_bytes=int(mib * 2**20))


def swap(x, axis, first):
    pairs = []
    for i in range(first, lax.axis_size(axis) - 1, 2):
        pairs += [(i, i + 1), (i + 1, i)]
    return lax.ppermute(x, axis, pairs)


def row_sum(x, ready):
    size = lax.axis_size("grp")
    got = []
    for by in range(1, size):
        if size & (size - 1) == 0:
            pairs = [(i, i ^ by) for i in range(size)]
        else:
            pairs = [(i, (i + by) % size) for i in range(size)]
        got.append(lax.ppermute(x, "grp", pairs))
    got, ready = lax.optimization_barrier((got, ready))
    return sum([y.astype(F32) for y in got], x.astype(F32)).astype(BF), ready


def per_device(nl, nt, ed, nc, ec, lists, src, tgt, own, sources, ef, es, nf, ns, mf, ms, cf, cs, pf, ps):
    slots, width = nl.shape
    edges = ed.shape[0]
    rim = lists.shape[2]
    owned, fan = sources.shape
    sources = sources.T
    row_nodes = owned * lax.axis_size("grp")
    extra = 2 * fan * (-(-row_nodes // (2 * width)))
    rows, block, cut = min(slots, 512), min(edges, 1024), min(edges, 512)
    shape = jax.ShapeDtypeStruct
    dma = pltpu.SemaphoreType.DMA
    *sent, nl, nt = pl.pallas_call(
        halo_kernel,
        out_shape=[pltpu.VMEM((rim, 2 * width), BF)] * 4 + like(nl, nt),
        in_specs=[HBM] * 3,
        out_specs=[VMEM] * 6,
        scratch_shapes=like(lists) + [dma((3,))],
        compiler_params=params(),
        cost_estimate=pl.CostEstimate(flops=8 * edges * slots * width, bytes_accessed=4 * slots * width, transcendentals=0),
        name="halo_rows",
    )(*(pltpu.with_memory_space_constraint(x, pltpu.HBM) for x in (nl, nt, lists)))
    got = [swap(sent[k], ("dom", "grp")[k // 2], k % 2) for k in range(4)]
    pre = pl.pallas_call(
        functools.partial(local_kernel, block=cut),
        out_shape=shape((edges, 2 * width), F32),
        in_specs=[VMEM] * 5,
        out_specs=VMEM,
        scratch_shapes=[pltpu.VMEM((2 * slots, 2 * width), BF)],
        compiler_params=params(),
        cost_estimate=pl.CostEstimate(
            flops=8 * edges * slots * width, bytes_accessed=8 * edges * width, transcendentals=0
        ),
        name="local",
    )(nl, nt, src, tgt, ef)
    first, part = pl.pallas_call(
        functools.partial(edge_kernel, block=min(edges, 2048), rows=256),
        out_shape=[shape((slots, 2 * width), BF), shape((row_nodes + extra, 2 * width), BF)],
        in_specs=[VMEM] * 11 + [SMEM] * 2 + [VMEM] * 5,
        out_specs=[VMEM] * 2,
        scratch_shapes=[
            pltpu.VMEM((4 * rim, 2 * width), BF),
            pltpu.VMEM((edges, 2 * width), BF),
            pltpu.VMEM((slots, 2 * width), BF),
        ],
        compiler_params=params(),
        name="edges",
    )(nl, nt, ed, src, tgt, own, sources, ef, es, nf, ns, nc, ec, *got, pre)
    weights, fixed, owner = pl.pallas_call(
        prepare_kernel,
        out_shape=[
            shape((14 * width, 2 * width), BF),
            shape((slots, 2 * width), F32),
            shape((slots, row_nodes), BF),
        ],
        in_specs=[VMEM] * 8,
        out_specs=[VMEM] * 3,
        compiler_params=params(),
        cost_estimate=pl.CostEstimate(
            flops=8 * slots * width * width, bytes_accessed=slots * width * 32, transcendentals=0
        ),
        name="prepare",
    )(first, own, mf, ms, cf, cs, pf, ps)
    summed, (weights, fixed, owner) = row_sum(part, (weights, fixed, owner))
    v1, v0 = swap(summed, "dom", 1), swap(summed, "dom", 0)
    given, outer, mine = pl.pallas_call(
        functools.partial(own_row_kernel, fan=fan),
        out_shape=[
            shape((fan * row_nodes, 2 * width), F32),
            shape((fan * row_nodes, 2 * row_nodes), BF),
            shape((row_nodes, 2 * width), F32),
        ],
        in_specs=[VMEM] * 2,
        out_specs=[VMEM] * 3,
        compiler_params=params(),
        cost_estimate=pl.CostEstimate(
            flops=4 * fan * row_nodes * row_nodes * width,
            bytes_accessed=slots * width * 32,
            transcendentals=0,
        ),
        name="own_row",
    )(summed, weights)
    return pl.pallas_call(
        functools.partial(coarse_kernel, fan=fan),
        out_shape=[shape((slots, width), BF)] * 2,
        in_specs=[VMEM] * 9 + [SMEM],
        out_specs=[HBM] * 2,
        scratch_shapes=[
            pltpu.VMEM((2 * row_nodes, 2 * width), BF),
            pltpu.VMEM((slots, width), BF),
            pltpu.VMEM((slots, width), BF),
            dma((2,)),
        ],
        compiler_params=params(),
        name="coarse",
    )(v0, v1, given, outer, mine, weights, fixed, owner, first, nc)


def solution(mesh):
    parts = ("dom", "grp")
    rows = P(parts, None)
    in_specs = (rows,) * 3 + (P(parts),) * 2 + (P(parts, None, None),) + (rows,) * 4 + (P(),) * 10
    return jax.shard_map(
        per_device, mesh=mesh, in_specs=in_specs, out_specs=(rows, rows), check_vma=False
    )
```

```python
import functools

import jax
import jax.numpy as jnp
from jax import lax
from jax.experimental import pallas as pl
from jax.experimental.pallas import tpu as pltpu
from jax.sharding import PartitionSpec as P

BF = jnp.bfloat16
F32 = jnp.float32
I16 = jnp.int16
I32 = jnp.int32
HBM = pl.BlockSpec(memory_space=pltpu.HBM)
SMEM = pl.BlockSpec(memory_space=pltpu.SMEM)
VMEM = pl.BlockSpec(memory_space=pltpu.VMEM)
LANES = 128
ORDER = (0, 1, 2, 3)
PEERS = (2, 1, 3)


def mm(a, b):
    return jnp.dot(a, b, preferred_element_type=F32)


def twice(weight):
    zero = jnp.zeros_like(weight)
    return jnp.concatenate(
        [jnp.concatenate([weight, zero], 1), jnp.concatenate([zero, weight], 1)], 0
    )


def centred(weight):
    weight = weight.astype(F32)
    return (weight - jnp.mean(weight, axis=1, keepdims=True)).astype(BF)


def averaging(width):
    return twice(jnp.full((width, width), 1.0 / width, BF))


def column(row):
    count = row.shape[1]
    parts = [
        jnp.broadcast_to(row[:, k : k + LANES], (LANES, LANES)).T for k in range(0, count, LANES)
    ]
    return jnp.concatenate(parts, 0).astype(I16)


def picks(col, count):
    lane = lax.broadcasted_iota(I32, (1, LANES), 1).astype(I16)
    one, zero = jnp.ones((), BF), jnp.zeros((), BF)
    return [
        jnp.where(col == jnp.broadcast_to(lane + jnp.asarray(k, I16), col.shape), one, zero)
        for k in range(0, count, LANES)
    ]


def row_picks(row, count, begin=0):
    place = (lax.broadcasted_iota(I32, (count, LANES), 0) + begin).astype(I16)
    one, zero = jnp.ones((), BF), jnp.zeros((), BF)
    parts = []
    for k in range(0, row.shape[1], LANES):
        few = jnp.broadcast_to(row[:, k : k + LANES], (16, LANES)).astype(I16)
        parts.append(jnp.where(jnp.concatenate([few] * (count // 16), 0) == place, one, zero))
    return jnp.concatenate(parts, 1)


def activated(pre):
    width = pre.shape[1] // 2
    value, tangent = pre[:, :width], pre[:, width:]
    gate = 0.5 + 0.5 * jnp.tanh(0.5 * value)
    hidden = value * gate
    slope = gate + hidden * (1.0 - gate)
    return jnp.concatenate([hidden, tangent * slope], 1)


def normed(pre, second, ones):
    width = pre.shape[1] // 2
    both = mm(activated(pre).astype(BF), second)
    value, tangent = both[:, :width], both[:, width:]
    stats = mm(jnp.concatenate([value * value, value * tangent], 1).astype(BF), ones)
    scale = lax.rsqrt(stats[:, :width] + 1e-05)
    return value * scale, scale * (tangent - value * (scale * scale * stats[:, width:]))


def fetch(pairs, sems):
    copies = [pltpu.make_async_copy(src, dst, sems.at[k]) for k, (src, dst) in enumerate(pairs)]
    for copy in copies:
        copy.start()
    return copies


def halo_kernel(nl, nt, lists, o0, o1, o2, o3, nl_v, nt_v, lists_v, sems, *, order):
    for copy in fetch([(lists, lists_v), (nl, nl_v), (nt, nt_v)], sems):
        copy.wait()
    slots = nl.shape[0]
    paired = jnp.concatenate([nl_v[...], nt_v[...]], 1)
    even = (lax.rem(lax.axis_index("dom"), 2) == 0, lax.rem(lax.axis_index("grp"), 2) == 0)
    for k, out in zip(order, (o0, o1, o2, o3)):
        base = k // 2 * 2
        up = even[k // 2] if k % 2 == 0 else jnp.logical_not(even[k // 2])
        row = jnp.where(up, lists_v[0, base : base + 1, :], lists_v[0, base + 1 : base + 2, :])
        selector = jnp.concatenate(picks(column(row), slots), 1)
        out[...] = mm(selector, paired).astype(BF)


def local_kernel(nl, nt, src, tgt, ef, pre_o, table, *, block):
    slots, width = nl.shape
    paired = jnp.concatenate([nl[...], nt[...]], 1)
    table[0:slots, :] = mm(paired, twice(ef[width : 2 * width, :])).astype(BF)
    table[slots:, :] = mm(paired, twice(ef[2 * width :, :])).astype(BF)
    for begin in range(0, pre_o.shape[0], block):
        at = slice(begin, begin + block)
        selector = jnp.concatenate(
            picks(column(src[0:1, at]), slots) + picks(column(tgt[0:1, at]), slots), 1
        )
        pre_o[at, :] = mm(selector, table[...])


def edge_kernel(nl_v, nt_v, ed_v, src_v, tgt_v, own_v, sources_v, ef_v, es_v, nf_v, ns_v, nc, ec,
                h0, h1, h2, h3, pre, first_o, part_o, table, pairs, sums, *, block, rows, order):
    slots, width = nl_v.shape
    edges = ed_v.shape[0]
    rim = h0.shape[0]
    weight = twice(ef_v[width : 2 * width, :])
    odd = (lax.rem(lax.axis_index("dom"), 2), lax.rem(lax.axis_index("grp"), 2))
    for k, got in zip(order, (h0, h1, h2, h3)):
        place = k // 2 * 2 + (odd[k // 2] if k % 2 else 1 - odd[k // 2])
        at = pl.ds(pl.multiple_of(place * rim, rim), rim)
        table[at, :] = mm(got[...], weight).astype(BF)
    second = twice(centred(es_v[...]))
    ones = averaging(width)
    own_weight = ef_v[0:width, :]
    for begin in range(0, edges, block):
        at = slice(begin, begin + block)
        selector = jnp.concatenate(picks(column(src_v[0:1, at] - slots), 4 * rim), 1)
        mine = ed_v[at, :]
        given = pre[at, :] + mm(selector, table[...])
        given = jnp.concatenate([given[:, :width] + mm(mine, own_weight), given[:, width:]], 1)
        value, tangent = normed(given, second, ones)
        pairs[at, :] = jnp.concatenate([mine.astype(F32) + value, tangent], 1).astype(BF)
    target = jnp.where(lax.broadcasted_iota(I32, (1, edges), 1) < ec[0], tgt_v[...], -1)
    owner = jnp.where(lax.broadcasted_iota(I32, (1, slots), 1) < nc[0], own_v[...], -1)
    fixed = twice(nf_v[0:width, :])
    added = twice(nf_v[width:, :])
    second = twice(centred(ns_v[...]))
    fan, owned = sources_v.shape
    row_nodes = owned * lax.axis_size("grp")
    for begin in range(0, slots, rows):
        sums[begin : begin + rows, :] = mm(row_picks(target, rows, begin), pairs[...]).astype(BF)
    paired = jnp.concatenate([nl_v[...], nt_v[...]], 1)
    value, tangent = normed(mm(paired, fixed) + mm(sums[...], added), second, ones)
    first = (paired.astype(F32) + jnp.concatenate([value, tangent], 1)).astype(BF)
    first_o[...] = first
    part_o[0:row_nodes, :] = mm(row_picks(owner, row_nodes), first).astype(BF)
    high = (sources_v[...] // 256).astype(F32).astype(BF)
    low = lax.rem(sources_v[...], 256).astype(F32).astype(BF)
    lane = lax.broadcasted_iota(I32, (owned, 2 * width), 1)
    spot = lax.broadcasted_iota(I32, (owned, 2 * width), 0) + lax.axis_index("grp") * owned
    for k in range((part_o.shape[0] - row_nodes) // (2 * fan)):
        place = jnp.where(lane + k * 2 * width == spot, jnp.ones((), F32), jnp.zeros((), F32)).astype(BF)
        base = row_nodes + k * 2 * fan
        part_o[base : base + 2 * fan, :] = jnp.concatenate([mm(high, place), mm(low, place)], 0).astype(BF)


def prepare_kernel(first, own, mf, ms, cf, cs, pf, ps, weights_o, fixed_o, owner_o):
    width = mf.shape[1]
    size = 2 * width
    stack = (
        twice(mf[0:width, :]),
        twice(mf[width:, :]),
        twice(mm(ms[...], cf[width:, :]).astype(BF)),
        twice(cf[0:width, :]),
        twice(centred(cs[...])),
        twice(pf[width:, :]),
        twice(centred(ps[...])),
    )
    for k, weight in enumerate(stack):
        weights_o[k * size : (k + 1) * size, :] = weight
    fixed_o[...] = mm(first[...], twice(pf[0:width, :]))
    owner_o[...] = jnp.concatenate(picks(column(own[...]), owner_o.shape[1]), 1)


def own_row_kernel(summed, weights, given_o, outer_o, mine_o, *, fan):
    row_nodes, size = mine_o.shape
    mine = summed[0:row_nodes, :]
    table = mm(mine, weights[0:size, :]).astype(BF)
    received = mm(mine, weights[size : 2 * size, :])
    for begin in range(0, row_nodes, LANES):
        chunk, lanes = divmod(begin, size)
        base = row_nodes + chunk * 2 * fan
        spots = summed[base : base + 2 * fan, lanes : lanes + LANES].astype(F32)
        spots = (spots[0:fan, :] * 256.0 + spots[fan:, :]).astype(I32)
        spots = jnp.concatenate([column(spots[j : j + 1, :]) for j in range(fan)], 0)
        blocks = picks(spots, 3 * row_nodes)
        few = row_nodes // LANES
        at = slice(begin * fan, (begin + LANES) * fan)
        got = received[begin : begin + LANES, :]
        given_o[at, :] = mm(jnp.concatenate(blocks[few : 2 * few], 1), table) + jnp.concatenate([got] * fan, 0)
        outer_o[at, :] = jnp.concatenate(blocks[:few] + blocks[2 * few :], 1)
    mine_o[...] = mm(mine, weights[3 * size : 4 * size, :])


def coarse_kernel(v0, v1, given, outer, mine, weights, fixed, owner, first, nc,
                  node_o, tangent_o, table, node_v, tangent_v, out_sems, *, fan):
    slots, width = node_o.shape
    row_nodes, size = mine.shape
    held = [weights[k * size : (k + 1) * size, :] for k in range(7)]
    ones = averaging(width)
    odd = lax.rem(lax.axis_index("dom"), 2)
    for k, got in enumerate((v0, v1)):
        place = odd if k else 1 - odd
        at = pl.ds(pl.multiple_of(place * row_nodes, row_nodes), row_nodes)
        table[at, :] = mm(got[0:row_nodes, :], held[0]).astype(BF)
    hidden = activated(given[...] + mm(outer[...], table[...]))
    sums = []
    for begin in range(0, row_nodes, LANES):
        part = [hidden[begin * fan + j * LANES : begin * fan + (j + 1) * LANES, :] for j in range(fan)]
        sums.append(sum(part))
    hidden = jnp.concatenate(sums, 0)
    large = hidden.astype(BF)
    small = (hidden - large.astype(F32)).astype(BF)
    value, tangent = normed(mine[...] + mm(large, held[2]) + mm(small, held[2]), held[4], ones)
    updated = jnp.concatenate([value, tangent], 1).astype(BF)
    brought = mm(updated, held[5]).astype(BF)
    value, tangent = normed(fixed[...] + mm(owner[...], brought), held[6], ones)
    base = first[...].astype(F32)
    valid = lax.broadcasted_iota(I32, (slots, 1), 0) < nc[0]
    node_v[...] = jnp.where(valid, base[:, :width] + value, 0.0).astype(BF)
    tangent_v[...] = jnp.where(valid, base[:, width:] + tangent, 0.0).astype(BF)
    for copy in fetch([(node_v, node_o), (tangent_v, tangent_o)], out_sems):
        copy.wait()


def like(*arrays):
    return [pltpu.VMEM(a.shape, a.dtype) for a in arrays]


def params(mib=40):
    return pltpu.CompilerParams(vmem_limit_bytes=int(mib * 2**20))


def swap(x, axis, first):
    pairs = []
    for i in range(first, lax.axis_size(axis) - 1, 2):
        pairs += [(i, i + 1), (i + 1, i)]
    return lax.ppermute(x, axis, pairs)


def row_sum(x, ready):
    size = lax.axis_size("grp")
    got = []
    for by in PEERS if size == len(PEERS) + 1 else range(1, size):
        if size & (size - 1) == 0:
            pairs = [(i, i ^ by) for i in range(size)]
        else:
            pairs = [(i, (i + by) % size) for i in range(size)]
        got.append(lax.ppermute(x, "grp", pairs))
    got, ready = lax.optimization_barrier((got, ready))
    return sum([y.astype(F32) for y in got], x.astype(F32)).astype(BF), ready


def per_device(nl, nt, ed, nc, ec, lists, src, tgt, own, sources, ef, es, nf, ns, mf, ms, cf, cs, pf, ps):
    slots, width = nl.shape
    edges = ed.shape[0]
    rim = lists.shape[2]
    owned, fan = sources.shape
    sources = sources.T
    row_nodes = owned * lax.axis_size("grp")
    extra = 2 * fan * (-(-row_nodes // (2 * width)))
    rows, block, cut = min(slots, 512), min(edges, 1024), min(edges, 512)
    shape = jax.ShapeDtypeStruct
    dma = pltpu.SemaphoreType.DMA
    *sent, nl, nt = pl.pallas_call(
        functools.partial(halo_kernel, order=ORDER),
        out_shape=[pltpu.VMEM((rim, 2 * width), BF)] * 4 + like(nl, nt),
        in_specs=[HBM] * 3,
        out_specs=[VMEM] * 6,
        scratch_shapes=like(lists) + [dma((3,))],
        compiler_params=params(),
        cost_estimate=pl.CostEstimate(flops=8 * edges * slots * width, bytes_accessed=4 * slots * width, transcendentals=0),
        name="halo_rows",
    )(*(pltpu.with_memory_space_constraint(x, pltpu.HBM) for x in (nl, nt, lists)))
    got = [swap(x, ("dom", "grp")[k // 2], k % 2) for k, x in zip(ORDER, sent)]
    pre = pl.pallas_call(
        functools.partial(local_kernel, block=cut),
        out_shape=shape((edges, 2 * width), F32),
        in_specs=[VMEM] * 5,
        out_specs=VMEM,
        scratch_shapes=[pltpu.VMEM((2 * slots, 2 * width), BF)],
        compiler_params=params(),
        cost_estimate=pl.CostEstimate(
            flops=8 * edges * slots * width, bytes_accessed=8 * edges * width, transcendentals=0
        ),
        name="local",
    )(nl, nt, src, tgt, ef)
    first, part = pl.pallas_call(
        functools.partial(edge_kernel, block=min(edges, 2048), rows=256, order=ORDER),
        out_shape=[shape((slots, 2 * width), BF), shape((row_nodes + extra, 2 * width), BF)],
        in_specs=[VMEM] * 11 + [SMEM] * 2 + [VMEM] * 5,
        out_specs=[VMEM] * 2,
        scratch_shapes=[
            pltpu.VMEM((4 * rim, 2 * width), BF),
            pltpu.VMEM((edges, 2 * width), BF),
            pltpu.VMEM((slots, 2 * width), BF),
        ],
        compiler_params=params(),
        name="edges",
    )(nl, nt, ed, src, tgt, own, sources, ef, es, nf, ns, nc, ec, *got, pre)
    weights, fixed, owner = pl.pallas_call(
        prepare_kernel,
        out_shape=[
            shape((14 * width, 2 * width), BF),
            shape((slots, 2 * width), F32),
            shape((slots, row_nodes), BF),
        ],
        in_specs=[VMEM] * 8,
        out_specs=[VMEM] * 3,
        compiler_params=params(),
        cost_estimate=pl.CostEstimate(
            flops=8 * slots * width * width, bytes_accessed=slots * width * 32, transcendentals=0
        ),
        name="prepare",
    )(first, own, mf, ms, cf, cs, pf, ps)
    summed, (weights, fixed, owner) = row_sum(part, (weights, fixed, owner))
    v1, v0 = swap(summed, "dom", 1), swap(summed, "dom", 0)
    given, outer, mine = pl.pallas_call(
        functools.partial(own_row_kernel, fan=fan),
        out_shape=[
            shape((fan * row_nodes, 2 * width), F32),
            shape((fan * row_nodes, 2 * row_nodes), BF),
            shape((row_nodes, 2 * width), F32),
        ],
        in_specs=[VMEM] * 2,
        out_specs=[VMEM] * 3,
        compiler_params=params(),
        cost_estimate=pl.CostEstimate(
            flops=4 * fan * row_nodes * row_nodes * width,
            bytes_accessed=slots * width * 32,
            transcendentals=0,
        ),
        name="own_row",
    )(summed, weights)
    return pl.pallas_call(
        functools.partial(coarse_kernel, fan=fan),
        out_shape=[shape((slots, width), BF)] * 2,
        in_specs=[VMEM] * 9 + [SMEM],
        out_specs=[HBM] * 2,
        scratch_shapes=[
            pltpu.VMEM((2 * row_nodes, 2 * width), BF),
            pltpu.VMEM((slots, width), BF),
            pltpu.VMEM((slots, width), BF),
            dma((2,)),
        ],
        compiler_params=params(),
        name="coarse",
    )(v0, v1, given, outer, mine, weights, fixed, owner, first, nc)


def solution(mesh):
    parts = ("dom", "grp")
    rows = P(parts, None)
    in_specs = (rows,) * 3 + (P(parts),) * 2 + (P(parts, None, None),) + (rows,) * 4 + (P(),) * 10
    return jax.shard_map(
        per_device, mesh=mesh, in_specs=in_specs, out_specs=(rows, rows), check_vma=False
    )
```

```python
import functools

import jax
import jax.numpy as jnp
from jax import lax
from jax.experimental import pallas as pl
from jax.experimental.pallas import tpu as pltpu
from jax.sharding import PartitionSpec as P

BF = jnp.bfloat16
F32 = jnp.float32
I16 = jnp.int16
I32 = jnp.int32
HBM = pl.BlockSpec(memory_space=pltpu.HBM)
SMEM = pl.BlockSpec(memory_space=pltpu.SMEM)
VMEM = pl.BlockSpec(memory_space=pltpu.VMEM)
LANES = 128
ORDER = (0, 1, 2, 3)
PEERS = (1, 2, 3)


def mm(a, b):
    return jnp.dot(a, b, preferred_element_type=F32)


def twice(weight):
    zero = jnp.zeros_like(weight)
    return jnp.concatenate(
        [jnp.concatenate([weight, zero], 1), jnp.concatenate([zero, weight], 1)], 0
    )


def centred(weight):
    weight = weight.astype(F32)
    return (weight - jnp.mean(weight, axis=1, keepdims=True)).astype(BF)


def averaging(width):
    return twice(jnp.full((width, width), 1.0 / width, BF))


def column(row):
    count = row.shape[1]
    parts = [
        jnp.broadcast_to(row[:, k : k + LANES], (LANES, LANES)).T for k in range(0, count, LANES)
    ]
    return jnp.concatenate(parts, 0).astype(I16)


def picks(col, count):
    lane = lax.broadcasted_iota(I32, (1, LANES), 1).astype(I16)
    one, zero = jnp.ones((), BF), jnp.zeros((), BF)
    return [
        jnp.where(col == jnp.broadcast_to(lane + jnp.asarray(k, I16), col.shape), one, zero)
        for k in range(0, count, LANES)
    ]


def row_picks(row, count, begin=0):
    place = (lax.broadcasted_iota(I32, (count, LANES), 0) + begin).astype(I16)
    one, zero = jnp.ones((), BF), jnp.zeros((), BF)
    parts = []
    for k in range(0, row.shape[1], LANES):
        few = jnp.broadcast_to(row[:, k : k + LANES], (16, LANES)).astype(I16)
        parts.append(jnp.where(jnp.concatenate([few] * (count // 16), 0) == place, one, zero))
    return jnp.concatenate(parts, 1)


def activated(pre):
    width = pre.shape[1] // 2
    value, tangent = pre[:, :width], pre[:, width:]
    gate = 0.5 + 0.5 * jnp.tanh(0.5 * value)
    hidden = value * gate
    slope = gate + hidden * (1.0 - gate)
    return jnp.concatenate([hidden, tangent * slope], 1)


def normed(pre, second, ones):
    width = pre.shape[1] // 2
    both = mm(activated(pre).astype(BF), second)
    value, tangent = both[:, :width], both[:, width:]
    stats = mm(jnp.concatenate([value * value, value * tangent], 1).astype(BF), ones)
    scale = lax.rsqrt(stats[:, :width] + 1e-05)
    return value * scale, scale * (tangent - value * (scale * scale * stats[:, width:]))


def fetch(pairs, sems):
    copies = [pltpu.make_async_copy(src, dst, sems.at[k]) for k, (src, dst) in enumerate(pairs)]
    for copy in copies:
        copy.start()
    return copies


def halo_kernel(nl, nt, lists, o0, o1, o2, nl_v, nt_v, lists_v, sems):
    for copy in fetch([(lists, lists_v), (nl, nl_v), (nt, nt_v)], sems):
        copy.wait()
    slots = nl.shape[0]
    paired = jnp.concatenate([nl_v[...], nt_v[...]], 1)
    even = (lax.rem(lax.axis_index("dom"), 2) == 0, lax.rem(lax.axis_index("grp"), 2) == 0)
    rim = o0.shape[0]
    for k, (out, at) in enumerate(((o0, 0), (o1, 0), (o2, 0), (o2, rim))):
        base = k // 2 * 2
        up = even[k // 2] if k % 2 == 0 else jnp.logical_not(even[k // 2])
        row = jnp.where(up, lists_v[0, base : base + 1, :], lists_v[0, base + 1 : base + 2, :])
        selector = jnp.concatenate(picks(column(row), slots), 1)
        out[at : at + rim, :] = mm(selector, paired).astype(BF)


def receiver_kernel(nl, nt, tgt, ef, pre_o, table, *, block):
    slots, width = nl.shape
    paired = jnp.concatenate([nl[...], nt[...]], 1)
    table[...] = mm(paired, twice(ef[2 * width :, :])).astype(BF)
    for begin in range(0, pre_o.shape[0], block):
        at = slice(begin, begin + block)
        selector = jnp.concatenate(picks(column(tgt[0:1, at]), slots), 1)
        pre_o[at, :] = mm(selector, table[...])


def sender_kernel(nl, nt, src, ef, pre, pre_o, table, *, block):
    slots, width = nl.shape
    paired = jnp.concatenate([nl[...], nt[...]], 1)
    table[...] = mm(paired, twice(ef[width : 2 * width, :])).astype(BF)
    for begin in range(0, pre_o.shape[0], block):
        at = slice(begin, begin + block)
        selector = jnp.concatenate(picks(column(src[0:1, at]), slots), 1)
        pre_o[at, :] = pre[at, :] + mm(selector, table[...])


def edge_kernel(nl_v, nt_v, ed_v, src_v, tgt_v, own_v, sources_v, ef_v, es_v, nf_v, ns_v, nc, ec,
                h0, h1, h2, h3, pre, first_o, part_o, table, pairs, sums, *, block, rows, order):
    slots, width = nl_v.shape
    edges = ed_v.shape[0]
    rim = h0.shape[0]
    weight = twice(ef_v[width : 2 * width, :])
    odd = (lax.rem(lax.axis_index("dom"), 2), lax.rem(lax.axis_index("grp"), 2))
    for k, got in zip(order, (h0, h1, h2, h3)):
        place = k // 2 * 2 + (odd[k // 2] if k % 2 else 1 - odd[k // 2])
        at = pl.ds(pl.multiple_of(place * rim, rim), rim)
        rows_in = got[0:rim, :]
        if k == 3:
            g = lax.axis_index("grp")
            rows_in = jnp.where((g == 0) | (g == lax.axis_size("grp") - 1), jnp.zeros_like(rows_in), rows_in)
        table[at, :] = mm(rows_in, weight).astype(BF)
    second = twice(centred(es_v[...]))
    ones = averaging(width)
    own_weight = ef_v[0:width, :]
    for begin in range(0, edges, block):
        at = slice(begin, begin + block)
        selector = jnp.concatenate(picks(column(src_v[0:1, at] - slots), 4 * rim), 1)
        mine = ed_v[at, :]
        given = pre[at, :] + mm(selector, table[...])
        given = jnp.concatenate([given[:, :width] + mm(mine, own_weight), given[:, width:]], 1)
        value, tangent = normed(given, second, ones)
        pairs[at, :] = jnp.concatenate([mine.astype(F32) + value, tangent], 1).astype(BF)
    target = jnp.where(lax.broadcasted_iota(I32, (1, edges), 1) < ec[0], tgt_v[...], -1)
    owner = jnp.where(lax.broadcasted_iota(I32, (1, slots), 1) < nc[0], own_v[...], -1)
    fixed = twice(nf_v[0:width, :])
    added = twice(nf_v[width:, :])
    second = twice(centred(ns_v[...]))
    fan, owned = sources_v.shape
    row_nodes = owned * lax.axis_size("grp")
    for begin in range(0, slots, rows):
        sums[begin : begin + rows, :] = mm(row_picks(target, rows, begin), pairs[...]).astype(BF)
    paired = jnp.concatenate([nl_v[...], nt_v[...]], 1)
    value, tangent = normed(mm(paired, fixed) + mm(sums[...], added), second, ones)
    first = (paired.astype(F32) + jnp.concatenate([value, tangent], 1)).astype(BF)
    first_o[...] = first
    part_o[0:row_nodes, :] = mm(row_picks(owner, row_nodes), first).astype(BF)
    high = (sources_v[...] // 256).astype(F32).astype(BF)
    low = lax.rem(sources_v[...], 256).astype(F32).astype(BF)
    lane = lax.broadcasted_iota(I32, (owned, 2 * width), 1)
    spot = lax.broadcasted_iota(I32, (owned, 2 * width), 0) + lax.axis_index("grp") * owned
    for k in range((part_o.shape[0] - row_nodes) // (2 * fan)):
        place = jnp.where(lane + k * 2 * width == spot, jnp.ones((), F32), jnp.zeros((), F32)).astype(BF)
        base = row_nodes + k * 2 * fan
        part_o[base : base + 2 * fan, :] = jnp.concatenate([mm(high, place), mm(low, place)], 0).astype(BF)


def prepare_kernel(first, own, mf, ms, cf, cs, pf, ps, weights_o, fixed_o, owner_o):
    width = mf.shape[1]
    size = 2 * width
    stack = (
        twice(mf[0:width, :]),
        twice(mf[width:, :]),
        twice(mm(ms[...], cf[width:, :]).astype(BF)),
        twice(cf[0:width, :]),
        twice(centred(cs[...])),
        twice(pf[width:, :]),
        twice(centred(ps[...])),
    )
    for k, weight in enumerate(stack):
        weights_o[k * size : (k + 1) * size, :] = weight
    fixed_o[...] = mm(first[...], twice(pf[0:width, :]))
    owner_o[...] = jnp.concatenate(picks(column(own[...]), owner_o.shape[1]), 1)


def own_row_kernel(summed, weights, given_o, outer_o, mine_o, *, fan):
    row_nodes, size = mine_o.shape
    mine = summed[0:row_nodes, :]
    table = mm(mine, weights[0:size, :]).astype(BF)
    received = mm(mine, weights[size : 2 * size, :])
    for begin in range(0, row_nodes, LANES):
        chunk, lanes = divmod(begin, size)
        base = row_nodes + chunk * 2 * fan
        spots = summed[base : base + 2 * fan, lanes : lanes + LANES].astype(F32)
        spots = (spots[0:fan, :] * 256.0 + spots[fan:, :]).astype(I32)
        spots = jnp.concatenate([column(spots[j : j + 1, :]) for j in range(fan)], 0)
        blocks = picks(spots, 3 * row_nodes)
        few = row_nodes // LANES
        at = slice(begin * fan, (begin + LANES) * fan)
        got = received[begin : begin + LANES, :]
        given_o[at, :] = mm(jnp.concatenate(blocks[few : 2 * few], 1), table) + jnp.concatenate([got] * fan, 0)
        outer_o[at, :] = jnp.concatenate(blocks[:few] + blocks[2 * few :], 1)
    mine_o[...] = mm(mine, weights[3 * size : 4 * size, :])


def coarse_kernel(v0, v1, given, outer, mine, weights, fixed, owner, first, nc,
                  node_o, tangent_o, table, node_v, tangent_v, out_sems, *, fan):
    slots, width = node_o.shape
    row_nodes, size = mine.shape
    held = [weights[k * size : (k + 1) * size, :] for k in range(7)]
    ones = averaging(width)
    odd = lax.rem(lax.axis_index("dom"), 2)
    for k, got in enumerate((v0, v1)):
        place = odd if k else 1 - odd
        at = pl.ds(pl.multiple_of(place * row_nodes, row_nodes), row_nodes)
        table[at, :] = mm(got[0:row_nodes, :], held[0]).astype(BF)
    hidden = activated(given[...] + mm(outer[...], table[...]))
    sums = []
    for begin in range(0, row_nodes, LANES):
        part = [hidden[begin * fan + j * LANES : begin * fan + (j + 1) * LANES, :] for j in range(fan)]
        sums.append(sum(part))
    hidden = jnp.concatenate(sums, 0)
    large = hidden.astype(BF)
    small = (hidden - large.astype(F32)).astype(BF)
    value, tangent = normed(mine[...] + mm(large, held[2]) + mm(small, held[2]), held[4], ones)
    updated = jnp.concatenate([value, tangent], 1).astype(BF)
    brought = mm(updated, held[5]).astype(BF)
    value, tangent = normed(fixed[...] + mm(owner[...], brought), held[6], ones)
    base = first[...].astype(F32)
    valid = lax.broadcasted_iota(I32, (slots, 1), 0) < nc[0]
    node_v[...] = jnp.where(valid, base[:, :width] + value, 0.0).astype(BF)
    tangent_v[...] = jnp.where(valid, base[:, width:] + tangent, 0.0).astype(BF)
    for copy in fetch([(node_v, node_o), (tangent_v, tangent_o)], out_sems):
        copy.wait()


def like(*arrays):
    return [pltpu.VMEM(a.shape, a.dtype) for a in arrays]


def params(mib=40):
    return pltpu.CompilerParams(vmem_limit_bytes=int(mib * 2**20))


def swap(x, axis, first):
    pairs = []
    for i in range(first, lax.axis_size(axis) - 1, 2):
        pairs += [(i, i + 1), (i + 1, i)]
    return lax.ppermute(x, axis, pairs)


def row_sum(x, ready):
    size = lax.axis_size("grp")
    got = []
    for by in PEERS if size == len(PEERS) + 1 else range(1, size):
        if size & (size - 1) == 0:
            pairs = [(i, i ^ by) for i in range(size)]
        else:
            pairs = [(i, (i + by) % size) for i in range(size)]
        got.append(lax.ppermute(x, "grp", pairs))
    got, ready = lax.optimization_barrier((got, ready))
    return sum([y.astype(F32) for y in got], x.astype(F32)).astype(BF), ready


def per_device(nl, nt, ed, nc, ec, lists, src, tgt, own, sources, ef, es, nf, ns, mf, ms, cf, cs, pf, ps):
    slots, width = nl.shape
    edges = ed.shape[0]
    rim = lists.shape[2]
    owned, fan = sources.shape
    sources = sources.T
    row_nodes = owned * lax.axis_size("grp")
    extra = 2 * fan * (-(-row_nodes // (2 * width)))
    rows, block, cut = min(slots, 512), min(edges, 1024), min(edges, 512)
    shape = jax.ShapeDtypeStruct
    dma = pltpu.SemaphoreType.DMA
    *sent, nl, nt = pl.pallas_call(
        halo_kernel,
        out_shape=[pltpu.VMEM((k * rim, 2 * width), BF) for k in (1, 1, 2)] + like(nl, nt),
        in_specs=[HBM] * 3,
        out_specs=[VMEM] * 5,
        scratch_shapes=like(lists) + [dma((3,))],
        compiler_params=params(),
        cost_estimate=pl.CostEstimate(flops=8 * edges * slots * width, bytes_accessed=4 * slots * width, transcendentals=0),
        name="halo_rows",
    )(*(pltpu.with_memory_space_constraint(x, pltpu.HBM) for x in (nl, nt, lists)))
    got = [swap(sent[0], "dom", 0), swap(sent[1], "dom", 1)]
    half_cost = pl.CostEstimate(
        flops=4 * edges * slots * width, bytes_accessed=8 * edges * width, transcendentals=0
    )
    pre = pl.pallas_call(
        functools.partial(receiver_kernel, block=cut),
        out_shape=shape((edges, 2 * width), F32),
        in_specs=[VMEM] * 4,
        out_specs=VMEM,
        scratch_shapes=[pltpu.VMEM((slots, 2 * width), BF)],
        compiler_params=params(),
        cost_estimate=half_cost,
        name="receivers",
    )(nl, nt, tgt, ef)
    if lax.axis_size("grp") == 4:
        near = swap(sent[2], "grp", 0)
        (*got, near), pre = lax.optimization_barrier(((*got, near), pre))
        far = lax.ppermute(near[rim:], "grp", [(i, i ^ 2) for i in range(4)])
    else:
        near, far = swap(sent[2][:rim], "grp", 0), swap(sent[2][rim:], "grp", 1)
    got += [near, far]
    pre = pl.pallas_call(
        functools.partial(sender_kernel, block=cut),
        out_shape=shape((edges, 2 * width), F32),
        in_specs=[VMEM] * 5,
        out_specs=VMEM,
        scratch_shapes=[pltpu.VMEM((slots, 2 * width), BF)],
        input_output_aliases={4: 0},
        compiler_params=params(),
        cost_estimate=half_cost,
        name="senders",
    )(nl, nt, src, ef, pre)
    (nc, ec), pre = lax.optimization_barrier(((nc, ec), pre))
    first, part = pl.pallas_call(
        functools.partial(edge_kernel, block=min(edges, 2048), rows=256, order=ORDER),
        out_shape=[shape((slots, 2 * width), BF), shape((row_nodes + extra, 2 * width), BF)],
        in_specs=[VMEM] * 11 + [SMEM] * 2 + [VMEM] * 5,
        out_specs=[VMEM] * 2,
        scratch_shapes=[
            pltpu.VMEM((4 * rim, 2 * width), BF),
            pltpu.VMEM((edges, 2 * width), BF),
            pltpu.VMEM((slots, 2 * width), BF),
        ],
        compiler_params=params(),
        name="edges",
    )(nl, nt, ed, src, tgt, own, sources, ef, es, nf, ns, nc, ec, *got, pre)
    weights, fixed, owner = pl.pallas_call(
        prepare_kernel,
        out_shape=[
            shape((14 * width, 2 * width), BF),
            shape((slots, 2 * width), F32),
            shape((slots, row_nodes), BF),
        ],
        in_specs=[VMEM] * 8,
        out_specs=[VMEM] * 3,
        compiler_params=params(),
        cost_estimate=pl.CostEstimate(
            flops=8 * slots * width * width, bytes_accessed=slots * width * 32, transcendentals=0
        ),
        name="prepare",
    )(first, own, mf, ms, cf, cs, pf, ps)
    summed, (weights, fixed, owner) = row_sum(part, (weights, fixed, owner))
    v1, v0 = swap(summed, "dom", 1), swap(summed, "dom", 0)
    given, outer, mine = pl.pallas_call(
        functools.partial(own_row_kernel, fan=fan),
        out_shape=[
            shape((fan * row_nodes, 2 * width), F32),
            shape((fan * row_nodes, 2 * row_nodes), BF),
            shape((row_nodes, 2 * width), F32),
        ],
        in_specs=[VMEM] * 2,
        out_specs=[VMEM] * 3,
        compiler_params=params(),
        cost_estimate=pl.CostEstimate(
            flops=4 * fan * row_nodes * row_nodes * width,
            bytes_accessed=slots * width * 32,
            transcendentals=0,
        ),
        name="own_row",
    )(summed, weights)
    return pl.pallas_call(
        functools.partial(coarse_kernel, fan=fan),
        out_shape=[shape((slots, width), BF)] * 2,
        in_specs=[VMEM] * 9 + [SMEM],
        out_specs=[HBM] * 2,
        scratch_shapes=[
            pltpu.VMEM((2 * row_nodes, 2 * width), BF),
            pltpu.VMEM((slots, width), BF),
            pltpu.VMEM((slots, width), BF),
            dma((2,)),
        ],
        compiler_params=params(),
        name="coarse",
    )(v0, v1, given, outer, mine, weights, fixed, owner, first, nc)


def solution(mesh):
    parts = ("dom", "grp")
    rows = P(parts, None)
    in_specs = (rows,) * 3 + (P(parts),) * 2 + (P(parts, None, None),) + (rows,) * 4 + (P(),) * 10
    return jax.shard_map(
        per_device, mesh=mesh, in_specs=in_specs, out_specs=(rows, rows), check_vma=False
    )
```

```python
import functools

import jax
import jax.numpy as jnp
from jax import lax
from jax.experimental import pallas as pl
from jax.experimental.pallas import tpu as pltpu
from jax.sharding import PartitionSpec as P

BF = jnp.bfloat16
F32 = jnp.float32
I16 = jnp.int16
I32 = jnp.int32
HBM = pl.BlockSpec(memory_space=pltpu.HBM)
SMEM = pl.BlockSpec(memory_space=pltpu.SMEM)
VMEM = pl.BlockSpec(memory_space=pltpu.VMEM)
LANES = 128
ORDER = (0, 1, 2, 3)
PEERS = (1, 2, 3)


def mm(a, b):
    return jnp.dot(a, b, preferred_element_type=F32)


def twice(weight):
    zero = jnp.zeros_like(weight)
    return jnp.concatenate(
        [jnp.concatenate([weight, zero], 1), jnp.concatenate([zero, weight], 1)], 0
    )


def centred(weight):
    weight = weight.astype(F32)
    return (weight - jnp.mean(weight, axis=1, keepdims=True)).astype(BF)


def averaging(width):
    return twice(jnp.full((width, width), 1.0 / width, BF))


def column(row):
    count = row.shape[1]
    parts = [
        jnp.broadcast_to(row[:, k : k + LANES], (LANES, LANES)).T for k in range(0, count, LANES)
    ]
    return jnp.concatenate(parts, 0).astype(I16)


def picks(col, count):
    lane = lax.broadcasted_iota(I32, (1, LANES), 1).astype(I16)
    one, zero = jnp.ones((), BF), jnp.zeros((), BF)
    return [
        jnp.where(col == jnp.broadcast_to(lane + jnp.asarray(k, I16), col.shape), one, zero)
        for k in range(0, count, LANES)
    ]


def row_picks(row, count, begin=0):
    place = (lax.broadcasted_iota(I32, (count, LANES), 0) + begin).astype(I16)
    one, zero = jnp.ones((), BF), jnp.zeros((), BF)
    parts = []
    for k in range(0, row.shape[1], LANES):
        few = jnp.broadcast_to(row[:, k : k + LANES], (16, LANES)).astype(I16)
        parts.append(jnp.where(jnp.concatenate([few] * (count // 16), 0) == place, one, zero))
    return jnp.concatenate(parts, 1)


def activated(pre):
    width = pre.shape[1] // 2
    value, tangent = pre[:, :width], pre[:, width:]
    gate = 0.5 + 0.5 * jnp.tanh(0.5 * value)
    hidden = value * gate
    slope = gate + hidden * (1.0 - gate)
    return jnp.concatenate([hidden, tangent * slope], 1)


def normed(pre, second, ones):
    width = pre.shape[1] // 2
    both = mm(activated(pre).astype(BF), second)
    value, tangent = both[:, :width], both[:, width:]
    stats = mm(jnp.concatenate([value * value, value * tangent], 1).astype(BF), ones)
    scale = lax.rsqrt(stats[:, :width] + 1e-05)
    return value * scale, scale * (tangent - value * (scale * scale * stats[:, width:]))


def fetch(pairs, sems):
    copies = [pltpu.make_async_copy(src, dst, sems.at[k]) for k, (src, dst) in enumerate(pairs)]
    for copy in copies:
        copy.start()
    return copies


def halo_kernel(nl, nt, lists, o0, o1, o2, nl_v, nt_v, lists_v, sems):
    for copy in fetch([(lists, lists_v), (nl, nl_v), (nt, nt_v)], sems):
        copy.wait()
    slots = nl.shape[0]
    paired = jnp.concatenate([nl_v[...], nt_v[...]], 1)
    even = (lax.rem(lax.axis_index("dom"), 2) == 0, lax.rem(lax.axis_index("grp"), 2) == 0)
    rim = o0.shape[0]
    for k, (out, at) in enumerate(((o0, 0), (o1, 0), (o2, 0), (o2, rim))):
        base = k // 2 * 2
        up = even[k // 2] if k % 2 == 0 else jnp.logical_not(even[k // 2])
        row = jnp.where(up, lists_v[0, base : base + 1, :], lists_v[0, base + 1 : base + 2, :])
        selector = jnp.concatenate(picks(column(row), slots), 1)
        out[at : at + rim, :] = mm(selector, paired).astype(BF)


def receiver_kernel(nl, nt, tgt, ef, pre_o, table, *, block):
    slots, width = nl.shape
    paired = jnp.concatenate([nl[...], nt[...]], 1)
    table[...] = mm(paired, twice(ef[2 * width :, :])).astype(BF)
    for begin in range(0, pre_o.shape[0], block):
        at = slice(begin, begin + block)
        selector = jnp.concatenate(picks(column(tgt[0:1, at]), slots), 1)
        pre_o[at, :] = mm(selector, table[...])


def sender_kernel(nl, nt, src, ef, pre, pre_o, table, *, block):
    slots, width = nl.shape
    paired = jnp.concatenate([nl[...], nt[...]], 1)
    table[...] = mm(paired, twice(ef[width : 2 * width, :])).astype(BF)
    for begin in range(0, pre_o.shape[0], block):
        at = slice(begin, begin + block)
        selector = jnp.concatenate(picks(column(src[0:1, at]), slots), 1)
        pre_o[at, :] = pre[at, :] + mm(selector, table[...])


def edge_kernel(nl_v, nt_v, ed_v, src_v, tgt_v, own_v, sources_v, ef_v, es_v, nf_v, ns_v, nc, ec,
                h0, h1, h2, h3, pre, first_o, part_o, table, pairs, sums, *, block, rows, order):
    slots, width = nl_v.shape
    edges = ed_v.shape[0]
    rim = h0.shape[0]
    weight = twice(ef_v[width : 2 * width, :])
    odd = (lax.rem(lax.axis_index("dom"), 2), lax.rem(lax.axis_index("grp"), 2))
    for k, got in zip(order, (h0, h1, h2, h3)):
        place = k // 2 * 2 + (odd[k // 2] if k % 2 else 1 - odd[k // 2])
        at = pl.ds(pl.multiple_of(place * rim, rim), rim)
        rows_in = got[0:rim, :]
        if k == 3:
            g = lax.axis_index("grp")
            rows_in = jnp.where((g == 0) | (g == lax.axis_size("grp") - 1), jnp.zeros_like(rows_in), rows_in)
        table[at, :] = mm(rows_in, weight).astype(BF)
    second = twice(centred(es_v[...]))
    ones = averaging(width)
    own_weight = ef_v[0:width, :]
    for begin in range(0, edges, block):
        at = slice(begin, begin + block)
        selector = jnp.concatenate(picks(column(src_v[0:1, at] - slots), 4 * rim), 1)
        mine = ed_v[at, :]
        given = pre[at, :] + mm(selector, table[...])
        given = jnp.concatenate([given[:, :width] + mm(mine, own_weight), given[:, width:]], 1)
        value, tangent = normed(given, second, ones)
        pairs[at, :] = jnp.concatenate([mine.astype(F32) + value, tangent], 1).astype(BF)
    target = jnp.where(lax.broadcasted_iota(I32, (1, edges), 1) < ec[0], tgt_v[...], -1)
    owner = jnp.where(lax.broadcasted_iota(I32, (1, slots), 1) < nc[0], own_v[...], -1)
    fixed = twice(nf_v[0:width, :])
    added = twice(nf_v[width:, :])
    second = twice(centred(ns_v[...]))
    fan, owned = sources_v.shape
    row_nodes = owned * lax.axis_size("grp")
    for begin in range(0, slots, rows):
        sums[begin : begin + rows, :] = mm(row_picks(target, rows, begin), pairs[...]).astype(BF)
    paired = jnp.concatenate([nl_v[...], nt_v[...]], 1)
    value, tangent = normed(mm(paired, fixed) + mm(sums[...], added), second, ones)
    first = (paired.astype(F32) + jnp.concatenate([value, tangent], 1)).astype(BF)
    first_o[...] = first
    part_o[0:row_nodes, :] = mm(row_picks(owner, row_nodes), first).astype(BF)
    high = (sources_v[...] // 256).astype(F32).astype(BF)
    low = lax.rem(sources_v[...], 256).astype(F32).astype(BF)
    lane = lax.broadcasted_iota(I32, (owned, 2 * width), 1)
    spot = lax.broadcasted_iota(I32, (owned, 2 * width), 0) + lax.axis_index("grp") * owned
    for k in range((part_o.shape[0] - row_nodes) // (2 * fan)):
        place = jnp.where(lane + k * 2 * width == spot, jnp.ones((), F32), jnp.zeros((), F32)).astype(BF)
        base = row_nodes + k * 2 * fan
        part_o[base : base + 2 * fan, :] = jnp.concatenate([mm(high, place), mm(low, place)], 0).astype(BF)


def prepare_kernel(first, own, mf, ms, cf, cs, pf, ps, weights_o, fixed_o, owner_o):
    width = mf.shape[1]
    size = 2 * width
    stack = (
        twice(mf[0:width, :]),
        twice(mf[width:, :]),
        twice(mm(ms[...], cf[width:, :]).astype(BF)),
        twice(cf[0:width, :]),
        twice(centred(cs[...])),
        twice(pf[width:, :]),
        twice(centred(ps[...])),
    )
    for k, weight in enumerate(stack):
        weights_o[k * size : (k + 1) * size, :] = weight
    fixed_o[...] = mm(first[...], twice(pf[0:width, :]))
    owner_o[...] = jnp.concatenate(picks(column(own[...]), owner_o.shape[1]), 1)


def own_row_kernel(summed, weights, given_o, outer_o, mine_o, *, fan):
    row_nodes, size = mine_o.shape
    mine = summed[0:row_nodes, :]
    table = mm(mine, weights[0:size, :]).astype(BF)
    received = mm(mine, weights[size : 2 * size, :])
    for begin in range(0, row_nodes, LANES):
        chunk, lanes = divmod(begin, size)
        base = row_nodes + chunk * 2 * fan
        spots = summed[base : base + 2 * fan, lanes : lanes + LANES].astype(F32)
        spots = (spots[0:fan, :] * 256.0 + spots[fan:, :]).astype(I32)
        spots = jnp.concatenate([column(spots[j : j + 1, :]) for j in range(fan)], 0)
        blocks = picks(spots, 3 * row_nodes)
        few = row_nodes // LANES
        at = slice(begin * fan, (begin + LANES) * fan)
        got = received[begin : begin + LANES, :]
        given_o[at, :] = mm(jnp.concatenate(blocks[few : 2 * few], 1), table) + jnp.concatenate([got] * fan, 0)
        outer_o[at, :] = jnp.concatenate(blocks[:few] + blocks[2 * few :], 1)
    mine_o[...] = mm(mine, weights[3 * size : 4 * size, :])


def coarse_kernel(v0, v1, given, outer, mine, weights, fixed, owner, first, nc,
                  node_o, tangent_o, table, node_v, tangent_v, out_sems, *, fan):
    slots, width = node_o.shape
    row_nodes, size = mine.shape
    held = [weights[k * size : (k + 1) * size, :] for k in range(7)]
    ones = averaging(width)
    odd = lax.rem(lax.axis_index("dom"), 2)
    for k, got in enumerate((v0, v1)):
        place = odd if k else 1 - odd
        at = pl.ds(pl.multiple_of(place * row_nodes, row_nodes), row_nodes)
        table[at, :] = mm(got[0:row_nodes, :], held[0]).astype(BF)
    hidden = activated(given[...] + mm(outer[...], table[...]))
    sums = []
    for begin in range(0, row_nodes, LANES):
        part = [hidden[begin * fan + j * LANES : begin * fan + (j + 1) * LANES, :] for j in range(fan)]
        sums.append(sum(part))
    hidden = jnp.concatenate(sums, 0)
    large = hidden.astype(BF)
    small = (hidden - large.astype(F32)).astype(BF)
    value, tangent = normed(mine[...] + mm(large, held[2]) + mm(small, held[2]), held[4], ones)
    updated = jnp.concatenate([value, tangent], 1).astype(BF)
    brought = mm(updated, held[5]).astype(BF)
    value, tangent = normed(fixed[...] + mm(owner[...], brought), held[6], ones)
    base = first[...].astype(F32)
    valid = lax.broadcasted_iota(I32, (slots, 1), 0) < nc[0]
    node_v[...] = jnp.where(valid, base[:, :width] + value, 0.0).astype(BF)
    tangent_v[...] = jnp.where(valid, base[:, width:] + tangent, 0.0).astype(BF)
    for copy in fetch([(node_v, node_o), (tangent_v, tangent_o)], out_sems):
        copy.wait()


def like(*arrays):
    return [pltpu.VMEM(a.shape, a.dtype) for a in arrays]


def params(mib=40):
    return pltpu.CompilerParams(vmem_limit_bytes=int(mib * 2**20))


def swap(x, axis, first):
    pairs = []
    for i in range(first, lax.axis_size(axis) - 1, 2):
        pairs += [(i, i + 1), (i + 1, i)]
    return lax.ppermute(x, axis, pairs)


def row_sum(x, ready):
    size = lax.axis_size("grp")
    got = []
    for by in PEERS if size == len(PEERS) + 1 else range(1, size):
        if size & (size - 1) == 0:
            pairs = [(i, i ^ by) for i in range(size)]
        else:
            pairs = [(i, (i + by) % size) for i in range(size)]
        got.append(lax.ppermute(x, "grp", pairs))
    got, ready = lax.optimization_barrier((got, ready))
    return sum([y.astype(F32) for y in got], x.astype(F32)).astype(BF), ready


def per_device(nl, nt, ed, nc, ec, lists, src, tgt, own, sources, ef, es, nf, ns, mf, ms, cf, cs, pf, ps):
    slots, width = nl.shape
    edges = ed.shape[0]
    rim = lists.shape[2]
    owned, fan = sources.shape
    sources = sources.T
    row_nodes = owned * lax.axis_size("grp")
    extra = 2 * fan * (-(-row_nodes // (2 * width)))
    rows, block, cut = min(slots, 512), min(edges, 1024), min(edges, 512)
    shape = jax.ShapeDtypeStruct
    dma = pltpu.SemaphoreType.DMA
    *sent, nl, nt = pl.pallas_call(
        halo_kernel,
        out_shape=[pltpu.VMEM((k * rim, 2 * width), BF) for k in (1, 1, 2)] + like(nl, nt),
        in_specs=[HBM] * 3,
        out_specs=[VMEM] * 5,
        scratch_shapes=like(lists) + [dma((3,))],
        compiler_params=params(),
        cost_estimate=pl.CostEstimate(flops=8 * edges * slots * width, bytes_accessed=4 * slots * width, transcendentals=0),
        name="halo_rows",
    )(*(pltpu.with_memory_space_constraint(x, pltpu.HBM) for x in (nl, nt, lists)))
    got = [swap(sent[0], "dom", 0), swap(sent[1], "dom", 1)]
    half_cost = pl.CostEstimate(
        flops=4 * edges * slots * width, bytes_accessed=8 * edges * width, transcendentals=0
    )
    pre = pl.pallas_call(
        functools.partial(receiver_kernel, block=cut),
        out_shape=shape((edges, 2 * width), F32),
        in_specs=[VMEM] * 4,
        out_specs=VMEM,
        scratch_shapes=[pltpu.VMEM((slots, 2 * width), BF)],
        compiler_params=params(),
        cost_estimate=half_cost,
        name="receivers",
    )(nl, nt, tgt, ef)
    if lax.axis_size("grp") == 4:
        near = swap(sent[2], "grp", 0)
        (*got, near), pre = lax.optimization_barrier(((*got, near), pre))
        far = lax.ppermute(near[rim:], "grp", [(i, i ^ 2) for i in range(4)])
    else:
        near, far = swap(sent[2][:rim], "grp", 0), swap(sent[2][rim:], "grp", 1)
    got += [near, far]
    pre = pl.pallas_call(
        functools.partial(sender_kernel, block=cut),
        out_shape=shape((edges, 2 * width), F32),
        in_specs=[VMEM] * 5,
        out_specs=VMEM,
        scratch_shapes=[pltpu.VMEM((slots, 2 * width), BF)],
        input_output_aliases={4: 0},
        compiler_params=params(),
        cost_estimate=half_cost,
        name="senders",
    )(nl, nt, src, ef, pre)
    (nc, ec), pre = lax.optimization_barrier(((nc, ec), pre))
    first, part = pl.pallas_call(
        functools.partial(edge_kernel, block=min(edges, 2048), rows=256, order=ORDER),
        out_shape=[shape((slots, 2 * width), BF), shape((row_nodes + extra, 2 * width), BF)],
        in_specs=[VMEM] * 11 + [SMEM] * 2 + [VMEM] * 5,
        out_specs=[VMEM] * 2,
        scratch_shapes=[
            pltpu.VMEM((4 * rim, 2 * width), BF),
            pltpu.VMEM((edges, 2 * width), BF),
            pltpu.VMEM((slots, 2 * width), BF),
        ],
        compiler_params=params(),
        name="edges",
    )(nl, nt, ed, src, tgt, own, sources, ef, es, nf, ns, nc, ec, *got, pre)
    weights, fixed, owner = pl.pallas_call(
        prepare_kernel,
        out_shape=[
            shape((14 * width, 2 * width), BF),
            shape((slots, 2 * width), F32),
            shape((slots, row_nodes), BF),
        ],
        in_specs=[VMEM] * 8,
        out_specs=[VMEM] * 3,
        compiler_params=params(),
        cost_estimate=pl.CostEstimate(
            flops=8 * slots * width * width, bytes_accessed=slots * width * 32, transcendentals=0
        ),
        name="prepare",
    )(first, own, mf, ms, cf, cs, pf, ps)
    summed, (weights, fixed, owner) = row_sum(part, (weights, fixed, owner))
    rows_sum = summed[:row_nodes]
    v1, v0 = swap(rows_sum, "dom", 1), swap(rows_sum, "dom", 0)
    given, outer, mine = pl.pallas_call(
        functools.partial(own_row_kernel, fan=fan),
        out_shape=[
            shape((fan * row_nodes, 2 * width), F32),
            shape((fan * row_nodes, 2 * row_nodes), BF),
            shape((row_nodes, 2 * width), F32),
        ],
        in_specs=[VMEM] * 2,
        out_specs=[VMEM] * 3,
        compiler_params=params(),
        cost_estimate=pl.CostEstimate(
            flops=4 * fan * row_nodes * row_nodes * width,
            bytes_accessed=slots * width * 32,
            transcendentals=0,
        ),
        name="own_row",
    )(summed, weights)
    return pl.pallas_call(
        functools.partial(coarse_kernel, fan=fan),
        out_shape=[shape((slots, width), BF)] * 2,
        in_specs=[VMEM] * 9 + [SMEM],
        out_specs=[HBM] * 2,
        scratch_shapes=[
            pltpu.VMEM((2 * row_nodes, 2 * width), BF),
            pltpu.VMEM((slots, width), BF),
            pltpu.VMEM((slots, width), BF),
            dma((2,)),
        ],
        compiler_params=params(),
        name="coarse",
    )(v0, v1, given, outer, mine, weights, fixed, owner, first, nc)


def solution(mesh):
    parts = ("dom", "grp")
    rows = P(parts, None)
    in_specs = (rows,) * 3 + (P(parts),) * 2 + (P(parts, None, None),) + (rows,) * 4 + (P(),) * 10
    return jax.shard_map(
        per_device, mesh=mesh, in_specs=in_specs, out_specs=(rows, rows), check_vma=False
    )
```
